32 devices in a mesh: row: 4 (over y, x), col: 8 (over z, core).
Axes of the slice: x: 2, y: 2, z: 4, core: 2. Of those that a mesh axis runs over, the one named last changes fastest.
Arguments:
- tile_counts: int32 [4, 8, 160, 128, 128], P('row', 'col'), may hold values from 0 to 1536, as said below
- tile_rows: int32 [4, 8, 160], P('row', 'col'), may hold values from 0 to 255, as said below
- tile_cols: int32 [4, 8, 160], P('row', 'col'), may hold values from 0 to 127
- panel: bfloat16 [131072, 128], P(('col', 'row')), may hold values from -0.059814453 to 0.059814453
Outputs:
- word_panel: float32 [131072, 128], P(('row', 'col'))
- context_panel: float32 [131072, 128], P(('col', 'row'))
The draws below stay inside these ranges and needn't reach their ends.
Inputs may be any that keep to these rules, and one draw needn't show every extreme that they name: `tile_counts`: on each device the occupied tiles come first: every slot at or after that device's number of occupied tiles holds only zeros, and some device has all 160 slots occupied. On each device the pairs (tile_rows, tile_cols) of the slots are distinct.
All inputs are finite; a program needn't handle non-finite values.
Results may differ from the reference program's by a relative error of at most 0.0029.
Values may be sent and summed in bfloat16 or wider, within the bound.
No kernel may reach another device: no remote copies, remote signals or barrier semaphores. Data moves between devices by JAX's collectives and lax.ppermute only.
A program may use at most 128 MiB of HBM per device.

```python
import math
import jax
import jax.numpy as jnp
from jax import lax

VOCAB = 131072
TILE = 128
PANEL = 128
NEG_SAMPLES = 15
TILES_DEV = 160
N_ROW = 4
N_COL = 8


def tile_layout(key):
    layout_key = jax.random.fold_in(key, 11)
    slot_total = VOCAB // (TILE * N_ROW) * (VOCAB // (TILE * N_COL))
    device_keys = jax.random.split(layout_key, N_ROW * N_COL)
    chosen = jax.vmap(lambda one_key: jax.random.permutation(one_key, slot_total)[:TILES_DEV])(device_keys)
    chosen = chosen.reshape(N_ROW, N_COL, TILES_DEV).astype(jnp.int32)
    band_cols = VOCAB // (TILE * N_COL)
    return (chosen // band_cols, chosen % band_cols)


def live_slots(key):
    live_key = jax.random.fold_in(key, 23)
    drawn = jax.random.randint(jax.random.fold_in(live_key, 1), (N_ROW * N_COL,), TILES_DEV // 8, TILES_DEV + 1)
    fullest = jax.random.randint(jax.random.fold_in(live_key, 2), (), 0, N_ROW * N_COL)
    drawn = jnp.where(jnp.arange(N_ROW * N_COL, dtype=jnp.int32) == fullest, TILES_DEV, drawn)
    return drawn.reshape(N_ROW, N_COL).astype(jnp.int32)


def draw_tile_rows(key, part):
    return tile_layout(key)[0]


def draw_tile_cols(key, part):
    return tile_layout(key)[1]


def draw_tile_counts(key, part):
    word_tiles, context_tiles = tile_layout(key)
    live = live_slots(key)
    band_rows = VOCAB // (TILE * N_ROW)
    band_cols = VOCAB // (TILE * N_COL)
    word_scale = jnp.left_shift(jnp.int32(1), jax.random.randint(jax.random.fold_in(key, 31), (VOCAB,), 0, 4))
    context_band = jnp.arange(VOCAB, dtype=jnp.int32) // (VOCAB // N_COL)
    context_scale = jnp.left_shift(jnp.int32(1), jax.random.randint(jax.random.fold_in(key, 37), (VOCAB,), 0, 3))
    context_scale = context_scale * (1 + 2 * context_band // (N_COL - 1))
    within = jnp.arange(TILE, dtype=jnp.int32)
    row_ids = jnp.arange(N_ROW, dtype=jnp.int32)[:, None, None, None]
    col_ids = jnp.arange(N_COL, dtype=jnp.int32)[None, :, None, None]
    word_ids = row_ids * band_rows * TILE + word_tiles[..., None] * TILE + within
    context_ids = col_ids * band_cols * TILE + context_tiles[..., None] * TILE + within
    spread = 3 * (N_ROW - 1)
    raw = jax.random.randint(jax.random.fold_in(key, 41), (N_ROW, N_COL, TILES_DEV, TILE, TILE), 0, 5 * spread)
    keep = raw // 5 < N_ROW - 1 + 2 * row_ids[..., None]
    alive = jnp.arange(TILES_DEV, dtype=jnp.int32)[None, None, :] < live[:, :, None]
    values = jnp.left_shift(jnp.int32(1), raw % 5) * word_scale[word_ids][..., :, None] * context_scale[context_ids][..., None, :]
    return jnp.where(keep & alive[..., None, None], values, 0).astype(jnp.int32)


def steps_of(rng, dims, shards, low, top_value):
    gain = 1.0
    for axis_at, parts in shards:
        draws = jax.random.uniform(jax.random.fold_in(jax.random.fold_in(rng, 6), axis_at), (parts,), jnp.float32, low / len(shards), top_value / len(shards))
        gain = gain * jnp.repeat(jnp.exp(draws), dims[axis_at] // parts).reshape((-1,) + (1,) * (len(dims) - 1 - axis_at))
    return gain


def bell_draw(rng, dims, scale, most, cuts=(), held_as=jnp.bfloat16):
    loudness = steps_of(rng, dims, cuts, -0.22, 0.18) if cuts else 1.0
    array = jax.random.normal(rng, dims, jnp.float32) * scale * loudness
    return jnp.minimum(jnp.maximum(array, -most), most).astype(held_as)


def setup_inputs(seed: int = 0) -> dict:
    keys = jax.random.split(jax.random.key(seed), 5)
    return {
        "tile_counts": draw_tile_counts(jax.random.fold_in(keys[4], 71), 0),
        "tile_rows": draw_tile_rows(jax.random.fold_in(keys[4], 71), 0),
        "tile_cols": draw_tile_cols(jax.random.fold_in(keys[4], 71), 0),
        "panel": bell_draw(keys[3], (VOCAB, PANEL), 0.01, 0.059814453, ((0, 32),)),
    }


def ppmi_tiles(counts, word_rows, context_cols, row_totals, context_powers, log_scale):
    counts_float = counts.astype(jnp.float32)
    word_log = jnp.log(jnp.maximum(row_totals[word_rows], 1.0))
    context_log = jnp.log(jnp.maximum(context_powers[context_cols], 1.0))
    pointwise = jnp.log(jnp.maximum(counts_float, 1.0)) + log_scale - word_log[:, :, None] - context_log[:, None, :]
    return jnp.where(counts > 0, jnp.maximum(pointwise, 0.0), 0.0).astype(jnp.bfloat16)


def reference(tile_counts, tile_rows, tile_cols, panel):
    band_rows = VOCAB // (TILE * N_ROW)
    band_cols = VOCAB // (TILE * N_COL)
    word_part = jnp.sum(tile_counts, axis=4).astype(jnp.float32)
    context_part = jnp.sum(tile_counts, axis=3).astype(jnp.float32)
    row_index = jnp.broadcast_to(jnp.arange(N_ROW, dtype=jnp.int32)[:, None, None], tile_rows.shape)
    col_index = jnp.broadcast_to(jnp.arange(N_COL, dtype=jnp.int32)[None, :, None], tile_cols.shape)
    row_totals = jnp.zeros((N_ROW, band_rows, TILE), jnp.float32).at[row_index, tile_rows].add(word_part)
    context_totals = jnp.zeros((N_COL, band_cols, TILE), jnp.float32).at[col_index, tile_cols].add(context_part)
    context_powers = context_totals ** 0.75
    log_scale = jnp.log(jnp.sum(context_powers)) - math.log(NEG_SAMPLES)
    panel_bands = panel.reshape(N_COL, band_cols, TILE, PANEL)

    def device_tiles(row_id, col_id):
        return ppmi_tiles(tile_counts[row_id, col_id], tile_rows[row_id, col_id], tile_cols[row_id, col_id],
                          row_totals[row_id], context_powers[col_id], log_scale)

    def word_band(row_id):
        def add_device(total, col_id):
            tiles = device_tiles(row_id, col_id)
            picked = panel_bands[col_id][tile_cols[row_id, col_id]]
            product = jnp.einsum("nij,njk->nik", tiles.astype(jnp.float32), picked.astype(jnp.float32))
            partial_sum = jax.ops.segment_sum(product, tile_rows[row_id, col_id], num_segments=band_rows)
            return total + partial_sum, None
        start = jnp.zeros((band_rows, TILE, PANEL), jnp.float32)
        return lax.scan(add_device, start, jnp.arange(N_COL, dtype=jnp.int32))[0]

    word_panel = lax.map(word_band, jnp.arange(N_ROW, dtype=jnp.int32))
    word_rounded = word_panel.astype(jnp.bfloat16)

    def context_band(col_id):
        def add_device(total, row_id):
            tiles = device_tiles(row_id, col_id)
            picked = word_rounded[row_id][tile_rows[row_id, col_id]]
            product = jnp.einsum("nji,njk->nik", tiles.astype(jnp.float32), picked.astype(jnp.float32))
            partial_sum = jax.ops.segment_sum(product, tile_cols[row_id, col_id], num_segments=band_cols)
            return total + partial_sum, None
        start = jnp.zeros((band_cols, TILE, PANEL), jnp.float32)
        return lax.scan(add_device, start, jnp.arange(N_ROW, dtype=jnp.int32))[0]

    context_panel = lax.map(context_band, jnp.arange(N_COL, dtype=jnp.int32))
    return word_panel.reshape(VOCAB, PANEL), (context_panel / TILE).reshape(VOCAB, PANEL)
```

```python
import functools
import math

import jax
import jax.numpy as jnp
from jax import lax
from jax.experimental import pallas as pl
from jax.experimental.pallas import tpu as pltpu
from jax.sharding import PartitionSpec as P

NEG_SAMPLES = 15
CHUNKS = 2
VMEM = 48 * 2**20
F32 = jnp.float32
BF16 = jnp.bfloat16


def params(**kwargs):
    return pltpu.CompilerParams(vmem_limit_bytes=VMEM, **kwargs)


def whole(shape):
    return pl.BlockSpec(shape, lambda *_: (0,) * len(shape))


ANY = pl.BlockSpec(memory_space=pl.ANY)


def cost(flops, moved):
    return pl.CostEstimate(flops=flops, bytes_accessed=moved, transcendentals=0)


def count_sums(counts, rows, cols, band_rows, band_cols):
    slots, tile, _ = counts.shape
    step = math.gcd(slots, 16)

    def kernel(rows_ref, cols_ref, counts_ref, word_ref, context_ref):
        at = pl.program_id(0)

        @pl.when(at == 0)
        def _():
            word_ref[...] = jnp.zeros_like(word_ref)
            context_ref[...] = jnp.zeros_like(context_ref)

        weights = jnp.concatenate(
            [jnp.full((8, tile), 32.0, BF16), jnp.ones((8, tile), BF16)], axis=1
        )
        for n in range(step):
            tile_counts = counts_ref[n]
            high = (tile_counts >> 5).astype(F32).astype(BF16)
            low = (tile_counts & 31).astype(F32).astype(BF16)
            context = jnp.dot(
                weights, jnp.concatenate([high, low], axis=0), preferred_element_type=F32
            )
            word = lax.dot_general(
                weights,
                jnp.concatenate([high, low], axis=1),
                (((1,), (1,)), ((), ())),
                preferred_element_type=F32,
            )
            row, col = rows_ref[at * step + n], cols_ref[at * step + n]
            word_ref[pl.ds(row, 1), :] += word[:1]
            context_ref[pl.ds(col, 1), :] += context[:1]

    return pl.pallas_call(
        kernel,
        grid_spec=pltpu.PrefetchScalarGridSpec(
            num_scalar_prefetch=2,
            grid=(slots // step,),
            in_specs=[pl.BlockSpec((step, tile, tile), lambda n, *_: (n, 0, 0))],
            out_specs=[whole((band_rows, tile)), whole((band_cols, tile))],
        ),
        out_shape=[
            jax.ShapeDtypeStruct((band_rows, tile), F32),
            jax.ShapeDtypeStruct((band_cols, tile), F32),
        ],
        compiler_params=params(),
        cost_estimate=cost(0, 4 * counts.size),
        name="count_sums",
    )(rows, cols, counts)


def smoothed(word_part, context_a, context_b):
    band_rows, tile = word_part.shape
    band_cols = context_a.shape[0]

    def kernel(word_ref, a_ref, b_ref, bundle_ref, log_ref):
        total = a_ref[...] + b_ref[...]
        root = jnp.sqrt(total)
        powers = root * jnp.sqrt(root)
        bundle_ref[:band_rows, :] = word_ref[...]
        bundle_ref[band_rows:, :] = jnp.sum(powers.reshape(band_cols // 8, 8, tile), axis=0)
        log_ref[...] = jnp.maximum(0.75 * jnp.log(total), 0.0)

    return pl.pallas_call(
        kernel,
        out_shape=[
            jax.ShapeDtypeStruct((band_rows + 8, tile), F32),
            jax.ShapeDtypeStruct((band_cols, tile), F32),
        ],
        compiler_params=params(),
        name="smoothed",
    )(word_part, context_a, context_b)


def ppmi(counts, rows, cols, bundle_a, bundle_b, context_log):
    slots, tile, _ = counts.shape
    band_rows = bundle_a.shape[0] - 8
    step = math.gcd(slots, 16)

    def kernel(rows_ref, cols_ref, counts_ref, a_ref, b_ref, log_ref, out_ref, word_log, shift):
        at = pl.program_id(0)

        @pl.when(at == 0)
        def _():
            totals = a_ref[:band_rows, :] + b_ref[:band_rows, :]
            word_log[...] = jnp.log(jnp.maximum(totals, 1.0))
            power = jnp.sum(a_ref[band_rows:, :] + b_ref[band_rows:, :], axis=0, keepdims=True)
            power = jnp.sum(power, axis=1, keepdims=True)
            shift[...] = (jnp.log(power) - math.log(NEG_SAMPLES)) - log_ref[...]

        for n in range(step):
            row, col = rows_ref[at * step + n], cols_ref[at * step + n]
            word = jnp.broadcast_to(word_log[pl.ds(row, 1), :], (tile, tile)).T
            logs = jnp.log(counts_ref[n].astype(F32))
            pointwise = logs + (shift[pl.ds(col, 1), :] - word)
            out_ref[n] = jnp.maximum(pointwise, 0.0).astype(BF16)

    return pl.pallas_call(
        kernel,
        grid_spec=pltpu.PrefetchScalarGridSpec(
            num_scalar_prefetch=2,
            grid=(slots // step,),
            in_specs=[
                pl.BlockSpec((step, tile, tile), lambda n, *_: (n, 0, 0)),
                whole(bundle_a.shape),
                whole(bundle_a.shape),
                whole(context_log.shape),
            ],
            out_specs=pl.BlockSpec((step, tile, tile), lambda n, *_: (n, 0, 0)),
            scratch_shapes=[
                pltpu.VMEM((band_rows, tile), F32),
                pltpu.VMEM(context_log.shape, F32),
            ],
        ),
        out_shape=jax.ShapeDtypeStruct(counts.shape, BF16),
        compiler_params=params(),
        cost_estimate=cost(0, 6 * counts.size),
        name="ppmi",
    )(rows, cols, counts, bundle_a, bundle_b, context_log)


def turn_panel(panel, tile):
    blocks, width = panel.shape[0] // tile, panel.shape[1]
    part = width // CHUNKS

    def kernel(in_ref, *out_refs):
        for n in range(blocks):
            turned = in_ref[n * tile : (n + 1) * tile, :].astype(F32).T.astype(BF16)
            for chunk, out_ref in enumerate(out_refs):
                out_ref[n] = turned[chunk * part : (chunk + 1) * part]

    return pl.pallas_call(
        kernel,
        out_shape=[jax.ShapeDtypeStruct((blocks, part, tile), BF16)] * CHUNKS,
        compiler_params=params(),
        name="turn_panel",
    )(panel)


def word_products(tiles, place, rows, cols, blocks, chips):
    slots, tile, _ = tiles.shape
    share, part, _ = blocks[0].shape
    slot_count, block_rows = 2 * chips - 1, place["block_rows"]
    step = math.gcd(slots, 32)
    grid = slots // step
    n_in = len(blocks)

    def kernel(rows_ref, cols_ref, valid_ref, tiles_ref, *refs):
        block_refs, outs = refs[:n_in], refs[n_in : n_in + slot_count]
        acc, band, sems = refs[n_in + slot_count :]
        at = pl.program_id(0)

        @pl.when(at == 0)
        def _():
            copies = [
                pltpu.make_async_copy(ref, band.at[pl.ds(n * share, share)], sems.at[n])
                for n, ref in enumerate(block_refs)
            ]
            for copy in copies:
                copy.start()
            for slot in range(slot_count):

                @pl.when(valid_ref[slot] == 1)
                def _():
                    acc[slot * block_rows : (slot + 1) * block_rows] = jnp.zeros(
                        (block_rows, part, tile), F32
                    )

            for copy in copies:
                copy.wait()

        for n in range(step):
            row, col = rows_ref[at * step + n], cols_ref[at * step + n]
            acc[row] += lax.dot_general(
                band[col], tiles_ref[n], (((1,), (1,)), ((), ())), preferred_element_type=F32
            )

        @pl.when(at == grid - 1)
        def _():
            for slot, out in enumerate(outs):

                @pl.when(valid_ref[slot] == 1)
                def _():
                    out[...] = acc[slot * block_rows : (slot + 1) * block_rows].astype(out.dtype)

    shape = (block_rows, part, tile)
    types = [BF16] * (chips - 1) + [F32] * chips
    outs = pl.pallas_call(
        kernel,
        grid_spec=pltpu.PrefetchScalarGridSpec(
            num_scalar_prefetch=3,
            grid=(grid,),
            in_specs=[pl.BlockSpec((step, tile, tile), lambda n, *_: (n, 0, 0))] + [ANY] * n_in,
            out_specs=[whole(shape)] * slot_count,
            scratch_shapes=[
                pltpu.VMEM((slot_count * block_rows, part, tile), F32),
                pltpu.VMEM((n_in * share, part, tile), BF16),
                pltpu.SemaphoreType.DMA((n_in,)),
            ],
        ),
        out_shape=[jax.ShapeDtypeStruct(shape, kind) for kind in types],
        compiler_params=params(),
        cost_estimate=cost(2 * slots * part * tile * tile, 2 * tiles.size + 4 * 2**20),
        name="word_products",
    )(rows, cols, place["valid"], tiles, *blocks)
    given = {distance: outs[chips - 1 - distance] for distance in range(1, chips)}
    kept = {distance: outs[chips - 1 + distance] for distance in range(1, chips)}
    return given, outs[chips - 1], kept


def context_products(tiles, place, rows, cols, blocks, band_cols):
    slots, tile, _ = tiles.shape
    block_rows, part, _ = blocks[0].shape
    slot_count = len(blocks)
    step = math.gcd(slots, 32)
    grid = slots // step
    half = band_cols // 2

    def kernel(rows_ref, cols_ref, valid_ref, tiles_ref, *refs):
        block_refs, (send, keep) = refs[:slot_count], refs[slot_count : slot_count + 2]
        acc, band, sems = refs[slot_count + 2 :]
        at = pl.program_id(0)

        @pl.when(at == 0)
        def _():
            for begin in (True, False):
                for slot, ref in enumerate(block_refs):

                    @pl.when(valid_ref[slot] == 1)
                    def _():
                        copy = pltpu.make_async_copy(
                            ref, band.at[pl.ds(slot * block_rows, block_rows)], sems.at[slot]
                        )
                        if begin:
                            copy.start()
                        else:
                            copy.wait()

                if begin:
                    acc[...] = jnp.zeros_like(acc)

        for n in range(step):
            row, col = rows_ref[at * step + n], cols_ref[at * step + n]
            acc[col] += jnp.dot(band[row], tiles_ref[n], preferred_element_type=F32)

        @pl.when(at == grid - 1)
        def _():
            send[...] = acc[half:].astype(BF16)
            keep[...] = acc[:half]

    shape = (half, part, tile)
    return pl.pallas_call(
        kernel,
        grid_spec=pltpu.PrefetchScalarGridSpec(
            num_scalar_prefetch=3,
            grid=(grid,),
            in_specs=[pl.BlockSpec((step, tile, tile), lambda n, *_: (n, 0, 0))]
            + [ANY] * slot_count,
            out_specs=[whole(shape)] * 2,
            scratch_shapes=[
                pltpu.VMEM((band_cols, part, tile), F32),
                pltpu.VMEM((slot_count * block_rows, part, tile), BF16),
                pltpu.SemaphoreType.DMA((slot_count,)),
            ],
        ),
        out_shape=[jax.ShapeDtypeStruct(shape, BF16), jax.ShapeDtypeStruct(shape, F32)],
        compiler_params=params(),
        cost_estimate=cost(2 * slots * part * tile * tile, 2 * tiles.size + 4 * 2**20),
        name="context_products",
    )(rows, cols, place["valid"], tiles, *blocks)


def turn_back(chunks, scale):
    blocks, part, tile = chunks[0][0].shape
    terms = [term for chunk in chunks for term in chunk]
    width = part * len(chunks)
    step = math.gcd(blocks, 8)

    def kernel(*refs):
        out_ref, reads = refs[-1], list(refs[:-1])
        for n in range(step):
            pieces, at = [], 0
            for chunk in chunks:
                pieces.append(sum(ref[n].astype(F32) for ref in reads[at : at + len(chunk)]))
                at += len(chunk)
            out_ref[n * tile : (n + 1) * tile, :] = jnp.concatenate(pieces, axis=0).T * scale

    return pl.pallas_call(
        kernel,
        grid=(blocks // step,),
        in_specs=[pl.BlockSpec((step, part, tile), lambda n: (n, 0, 0))] * len(terms),
        out_specs=pl.BlockSpec((step * tile, width), lambda n: (n, 0)),
        out_shape=jax.ShapeDtypeStruct((blocks * tile, width), F32),
        compiler_params=params(),
        cost_estimate=cost(0, 8 * blocks * tile * width),
        name="turn_back",
    )(*terms)


def shards(n_row, n_col, tile_counts, tile_rows, tile_cols, panel):
    counts, rows, cols = tile_counts[0, 0], tile_rows[0, 0], tile_cols[0, 0]
    tile = counts.shape[-1]
    share = panel.shape[0] // tile
    band_rows, band_cols = share * n_col, share * n_row
    chips, bits = n_col // 2, n_row.bit_length() - 1
    block_rows = 2 * share
    my_row, my_col = lax.axis_index("row"), lax.axis_index("col")
    chip, core = my_col // 2, my_col % 2

    def row_swap(x, step):
        pairs = []
        for r in range(n_row):
            for c in range(n_col):
                bit = step if c % 2 == 0 else bits - 1 - step
                pairs.append((r * n_col + c, (r ^ (1 << bit)) * n_col + c))
        return lax.ppermute(x, ("row", "col"), pairs)

    def core_swap(x, keep=lambda c, z: True):
        return lax.ppermute(
            x, "col", [(i, i ^ 1) for i in range(n_col) if keep(i % 2, i // 2)]
        )

    def along(x, keep):
        pairs = []
        for z in range(chips - 1):
            if keep(z):
                pairs.append((2 * z, 2 * z + 2))
                pairs.append((2 * (chips - 1 - z) + 1, 2 * (chips - 2 - z) + 1))
        return lax.ppermute(x, "col", pairs)

    distance = (rows // block_rows - chip) * jnp.where(core == 0, 1, -1)
    row_place = (distance + chips - 1) * block_rows + rows % block_rows
    slot_chip = (jnp.arange(2 * chips - 1) - (chips - 1)) * jnp.where(core == 0, 1, -1) + chip
    place = {
        "block_rows": block_rows,
        "valid": ((slot_chip >= 0) & (slot_chip < chips)).astype(jnp.int32),
    }
    differ = (cols // share) ^ my_row
    turned = sum(((differ >> b) & 1) << (bits - 1 - b) for b in range(bits))
    col_place = jnp.where(core == 0, turned, differ) * share + cols % share

    panel_parts = turn_panel(panel, tile)
    panel_blocks = []
    for part in panel_parts:
        blocks = {0: part}
        for step in range(bits):
            blocks.update(
                {
                    at | (1 << (bits - 1 - step)): row_swap(block, step)
                    for at, block in list(blocks.items())
                }
            )
        panel_blocks.append([blocks[at] for at in range(n_row)])

    word_part, context = count_sums(counts, rows, cols, band_rows, band_cols)
    for step in range(bits - 1):
        context = context + row_swap(context, step)
    bundle, context_log = smoothed(word_part, context, row_swap(context, bits - 1))
    bundle = bundle + core_swap(bundle)
    other = None
    for step in range(chips.bit_length() - 1):
        if other is not None:
            bundle = bundle + other
        other = lax.ppermute(bundle, "col", [(i, i ^ (2 << step)) for i in range(n_col)])
    tiles = ppmi(counts, rows, cols, bundle, other, context_log)

    word_chunks, context_chunks = [], []
    for chunk in range(CHUNKS):
        given, mine, kept = word_products(
            tiles, place, row_place, col_place, panel_blocks[chunk], chips
        )
        got = None
        for step in range(1, chips):
            far = chips - step
            passed = core_swap(
                given[far], lambda c, z, far=far: z >= far if c == 0 else z < chips - far
            )
            total = kept[far] + passed.astype(F32)
            if got is not None:
                total = total + got.astype(F32)
            got = along(total.astype(BF16), lambda z, step=step: z <= step - 1)
        mine = mine + got.astype(F32)
        mine = mine + core_swap(mine)
        word_chunks.append([lax.dynamic_slice_in_dim(mine, core * share, share)])
        rounded = mine.astype(BF16)
        near, swapped, block = [], [], rounded
        for step in range(1, chips):
            block = along(block, lambda z, step=step: z >= step - 1)
            near.append(block)
            swapped.append(core_swap(block))
        blocks = near[::-1] + [rounded] + swapped
        send, keep = context_products(tiles, place, row_place, col_place, blocks, band_cols)
        for step in range(bits):
            got = row_swap(send, step)
            if step < bits - 1:
                keep = keep + got.astype(F32)
                half = keep.shape[0] // 2
                send, keep = keep[half:].astype(BF16), keep[:half]
        context_chunks.append([keep, got])
    return turn_back(word_chunks, 1.0), turn_back(context_chunks, 1.0 / tile)


def solution(mesh):
    in_specs = (
        P("row", "col", None, None, None),
        P("row", "col", None),
        P("row", "col", None),
        P(("col", "row"), None),
    )
    out_specs = (P(("row", "col"), None), P(("col", "row"), None))
    body = functools.partial(shards, mesh.shape["row"], mesh.shape["col"])
    return jax.shard_map(body, mesh=mesh, in_specs=in_specs, out_specs=out_specs, check_vma=False)
```

```python
import functools
import math

import jax
import jax.numpy as jnp
from jax import lax
from jax.experimental import pallas as pl
from jax.experimental.pallas import tpu as pltpu
from jax.sharding import PartitionSpec as P

NEG_SAMPLES = 15
GROUPS = 2
PARTS = 2
F32 = jnp.float32
BF16 = jnp.bfloat16

ANY = pl.BlockSpec(memory_space=pl.ANY)
HBM = pl.BlockSpec(memory_space=pltpu.HBM)
IN_VMEM = pl.BlockSpec(memory_space=pltpu.VMEM)
IN_SMEM = pl.BlockSpec(memory_space=pltpu.SMEM)


def params(mib):
    return pltpu.CompilerParams(vmem_limit_bytes=mib * 2**20)


def cost(microseconds):
    return pl.CostEstimate(flops=0, bytes_accessed=int(microseconds * 3.69e6), transcendentals=0)


def in_hbm(x):
    return pltpu.with_memory_space_constraint(x, pltpu.HBM)


def over_tiles(slots, unroll, first, second):
    unroll = math.gcd(slots, unroll)

    def body(at, carry):
        found = [first(at * unroll + n) for n in range(unroll)]
        for n, one in enumerate(found):
            second(at * unroll + n, one)
        return carry

    lax.fori_loop(0, slots // unroll, body, 0)


def count_sums(counts, rows, cols, band_rows, band_cols, deps):
    slots, tile, _ = counts.shape
    pieces = math.gcd(slots, 10)
    piece = slots // pieces

    def kernel(counts_ref, rows_hbm, cols_hbm, *refs):
        word_ref, context_ref, held, rows_ref, cols_ref, sems = refs[len(deps) :]
        lists = [
            pltpu.make_async_copy(rows_hbm, rows_ref, sems.at[pieces]),
            pltpu.make_async_copy(cols_hbm, cols_ref, sems.at[pieces + 1]),
        ]

        def arriving(n):
            part = pl.ds(n * piece, piece)
            return pltpu.make_async_copy(counts_ref.at[part], held.at[part], sems.at[n])

        for copy in lists + [arriving(n) for n in range(pieces)]:
            copy.start()
        word_ref[...] = jnp.zeros_like(word_ref)
        context_ref[...] = jnp.zeros_like(context_ref)
        for copy in lists:
            copy.wait()

        def sums(n):
            values = held[n].astype(F32)
            return (
                jnp.sum(jnp.sum(values.T.reshape(tile // 8, 8, tile), axis=0), axis=0, keepdims=True),
                jnp.sum(jnp.sum(values.reshape(tile // 8, 8, tile), axis=0), axis=0, keepdims=True),
            )

        def add(n, found):
            word_ref[pl.ds(rows_ref[n], 1), :] += found[0]
            context_ref[pl.ds(cols_ref[n], 1), :] += found[1]

        def one_piece(at, carry):
            arriving(at).wait()
            over_tiles(
                piece, 16, lambda n: sums(at * piece + n), lambda n, found: add(at * piece + n, found)
            )
            return carry

        lax.fori_loop(0, pieces, one_piece, 0)

    return pl.pallas_call(
        kernel,
        in_specs=[HBM, ANY, ANY] + [ANY] * len(deps),
        out_specs=[IN_VMEM] * 2,
        out_shape=[
            jax.ShapeDtypeStruct((band_rows, tile), F32),
            jax.ShapeDtypeStruct((band_cols, tile), F32),
        ],
        scratch_shapes=[
            pltpu.VMEM(counts.shape, counts.dtype),
            pltpu.SMEM((slots,), jnp.int32),
            pltpu.SMEM((slots,), jnp.int32),
            pltpu.SemaphoreType.DMA((pieces + 2,)),
        ],
        compiler_params=params(48),
        cost_estimate=cost(0.01),
        name="count_sums",
    )(counts, rows, cols, *deps)


def smoothed(contexts):
    band_cols, tile = contexts[0].shape

    def kernel(*refs):
        power_ref, log_ref = refs[len(contexts) :]
        total = refs[0][...]
        for ref in refs[1 : len(contexts)]:
            total = total + ref[...]
        root = jnp.sqrt(total)
        powers = root * jnp.sqrt(root)
        power_ref[...] = jnp.sum(powers.reshape(band_cols // 8, 8, tile), axis=0)
        log_ref[...] = jnp.maximum(0.75 * jnp.log(total), 0.0)

    return pl.pallas_call(
        kernel,
        out_shape=[
            jax.ShapeDtypeStruct((8, tile), F32),
            jax.ShapeDtypeStruct((band_cols, tile), F32),
        ],
        compiler_params=params(16),
        name="smoothed",
    )(*contexts)


def turn_panel(panel, tile, group, deps):
    blocks, width = panel.shape[0] // tile, panel.shape[1]
    part = width // GROUPS

    def kernel(in_ref, *refs):
        out_ref = refs[-1]
        for n in range(blocks):
            turned = in_ref[n * tile : (n + 1) * tile, :].astype(F32).T.astype(BF16)
            out_ref[n] = turned[group * part : (group + 1) * part]

    return pl.pallas_call(
        kernel,
        in_specs=[IN_VMEM] + [ANY] * len(deps),
        out_specs=IN_VMEM,
        out_shape=jax.ShapeDtypeStruct((blocks, part, tile), BF16),
        compiler_params=params(16),
        name="turn_panel",
    )(panel, *deps)


def add_up(terms, count, width, dtypes, deps=(), other=None):
    tile = terms[0][0].shape[-1]
    n_terms = len(terms)

    def kernel(place_ref, *refs):
        outs = refs[n_terms + (other is not None) + len(deps) :]

        def write():
            total = refs[0][...].astype(F32)
            for ref in refs[1:n_terms]:
                total = total + ref[...].astype(F32)
            for out in outs:
                out[...] = total.astype(out.dtype)

        if other is None:
            write()
        else:
            pl.when(place_ref[0] < other[2])(write)

            @pl.when(place_ref[0] >= other[2])
            def _():
                outs[0][...] = refs[n_terms][...]

    shape = (count, width, tile)
    blocks = [pl.BlockSpec(shape, lambda n, _, at=at: (*at, 0)) for _, at in terms]
    arrays = [array for array, _ in terms]
    if other is None:
        place = jnp.zeros((1,), jnp.int32)
    else:
        place = other[1]
        blocks.append(pl.BlockSpec(shape, lambda n, _: (0, 0, 0)))
        arrays.append(other[0])
    return pl.pallas_call(
        kernel,
        grid_spec=pltpu.PrefetchScalarGridSpec(
            num_scalar_prefetch=1,
            grid=(1,),
            in_specs=blocks + [ANY] * len(deps),
            out_specs=[pl.BlockSpec(shape, lambda n, _: (0, 0, 0))] * len(dtypes),
        ),
        out_shape=[jax.ShapeDtypeStruct(shape, dtype) for dtype in dtypes],
        compiler_params=params(24),
        cost_estimate=cost(0.01),
        name="add_up",
    )(place, *arrays, *deps)


def word_products(index, blocks, chips, block_rows, tiles=None, source=None, deps=()):
    shape = (tiles if source is None else source[0]).shape
    slots, tile, _ = shape
    share, width, _ = blocks[0].shape
    slot_count = 2 * chips - 1
    n_in = len(blocks)
    chip_list = 3 * slots
    pieces = math.gcd(slots, 10)
    piece = slots // pieces
    n_powers = 0 if source is None else len(source[2])

    def kernel(index_ref, *refs):
        if source is None:
            tiles_ref, *refs = refs
        else:
            counts_hbm, first_ref, second_ref, *refs = refs
            power_refs, (log_ref, *refs) = refs[:n_powers], refs[n_powers:]
        block_refs, refs = refs[:n_in], refs[n_in + len(deps) :]
        if source is not None:
            tiles_ref, *refs = refs
        outs, refs = refs[:slot_count], refs[slot_count:]
        acc, band, sems, *refs = refs
        copies = [
            pltpu.make_async_copy(ref, band.at[pl.ds(n * share, share)], sems.at[n])
            for n, ref in enumerate(block_refs)
        ]
        for copy in copies:
            copy.start()
        acc[...] = jnp.zeros_like(acc)
        if source is not None:
            word_log, shift, counts_ref, count_sems = refs

            def arriving(n):
                part = pl.ds(n * piece, piece)
                return pltpu.make_async_copy(
                    counts_hbm.at[part], counts_ref.at[part], count_sems.at[n]
                )

            for n in range(pieces):
                arriving(n).start()
            rows = first_ref.shape[0]
            word_log[:rows] = jnp.log(jnp.maximum(first_ref[...], 1.0))
            word_log[rows:] = jnp.log(jnp.maximum(second_ref[...], 1.0))
            power = power_refs[0][...]
            for ref in power_refs[1:]:
                power = power + ref[...]
            power = jnp.sum(jnp.sum(power, axis=0, keepdims=True), axis=1, keepdims=True)
            shift[...] = (jnp.log(power) - math.log(NEG_SAMPLES)) - log_ref[...]
        for copy in copies:
            copy.wait()

        def product(n):
            if source is None:
                made = tiles_ref[n]
            else:
                word = word_log[pl.ds(index_ref[n], 1), :]
                word = jnp.broadcast_to(word, (tile, tile)).T
                context = shift[pl.ds(index_ref[slots + n], 1), :]
                pointwise = jnp.log(counts_ref[n].astype(F32)) + (context - word)
                made = jnp.maximum(pointwise, 0.0).astype(BF16)
                tiles_ref[n] = made
            return lax.dot_general(
                band[index_ref[2 * slots + n]],
                made,
                (((1,), (1,)), ((), ())),
                preferred_element_type=F32,
            )

        def add(n, found):
            acc[index_ref[n]] += found

        def one_piece(at, carry):
            if source is not None:
                arriving(at).wait()
            over_tiles(
                piece,
                16,
                lambda n: product(at * piece + n),
                lambda n, found: add(at * piece + n, found),
            )
            return carry

        lax.fori_loop(0, pieces, one_piece, 0)
        for slot, out in enumerate(outs):

            at = index_ref[chip_list + slot]

            @pl.when((at >= 0) & (at < chips))
            def _():
                out[...] = acc[pl.ds(at * block_rows, block_rows)].astype(out.dtype)

    out_shape = [
        pltpu.VMEM((block_rows, width, tile), F32 if slot == chips - 1 else BF16)
        for slot in range(slot_count)
    ]
    out_specs = [IN_VMEM] * slot_count
    scratch = [
        pltpu.VMEM((chips * block_rows, width, tile), F32),
        pltpu.VMEM((n_in * share, width, tile), BF16),
        pltpu.SemaphoreType.DMA((n_in,)),
    ]
    if source is None:
        operands, operand_specs = [tiles], [IN_VMEM]
    else:
        operands = [in_hbm(source[0]), *source[1], *source[2], source[3]]
        operand_specs = [HBM] + [IN_VMEM] * (len(operands) - 1)
    if source is not None:
        out_shape = [pltpu.VMEM(shape, BF16)] + out_shape
        out_specs = [IN_VMEM] + out_specs
        scratch += [
            pltpu.VMEM((2 * source[1][0].shape[0], tile), F32),
            pltpu.VMEM(source[3].shape, F32),
            pltpu.VMEM(shape, jnp.int32),
            pltpu.SemaphoreType.DMA((pieces,)),
        ]
    outs = pl.pallas_call(
        kernel,
        in_specs=[IN_SMEM] + operand_specs + [ANY] * (n_in + len(deps)),
        out_specs=out_specs,
        out_shape=out_shape,
        scratch_shapes=scratch,
        compiler_params=params(40 if source is not None else 32),
        cost_estimate=cost(0.01),
        name="word_products" if source is None else "ppmi_word_products",
    )(index, *operands, *blocks, *deps)
    if source is not None:
        tiles, *outs = outs
    given = {distance: outs[chips - 1 - distance] for distance in range(1, chips)}
    kept = {distance: outs[chips - 1 + distance] for distance in range(1, chips)}
    return tiles, given, outs[chips - 1], kept


def context_products(index, tiles, blocks, band_cols, deps):
    slots, tile, _ = tiles.shape
    block_rows, part, _ = blocks[0].shape
    slot_count = len(blocks)
    chips = (slot_count + 1) // 2
    half = band_cols // 2
    chip_list = 3 * slots

    def kernel(index_ref, tiles_ref, *refs):
        block_refs, refs = refs[:slot_count], refs[slot_count + len(deps) :]
        send, keep, acc, band, sems = refs

        def each_copy(act):
            for slot in range(slot_count):
                at = index_ref[chip_list + slot]

                @pl.when((at >= 0) & (at < chips))
                def _():
                    rows = pl.ds(at * block_rows, block_rows)
                    act(pltpu.make_async_copy(block_refs[slot], band.at[rows], sems.at[slot]))

        each_copy(lambda copy: copy.start())
        acc[...] = jnp.zeros_like(acc)
        each_copy(lambda copy: copy.wait())

        def product(n):
            return jnp.dot(band[index_ref[n]], tiles_ref[n], preferred_element_type=F32)

        def add(n, found):
            acc[index_ref[2 * slots + n]] += found

        over_tiles(slots, 16, product, add)
        send[...] = acc[half:].astype(BF16)
        keep[...] = acc[:half]

    shape = (half, part, tile)
    return pl.pallas_call(
        kernel,
        in_specs=[IN_SMEM, IN_VMEM] + [ANY] * (slot_count + len(deps)),
        out_specs=[IN_VMEM] * 2,
        out_shape=[jax.ShapeDtypeStruct(shape, BF16), jax.ShapeDtypeStruct(shape, F32)],
        scratch_shapes=[
            pltpu.VMEM((band_cols, part, tile), F32),
            pltpu.VMEM((chips * block_rows, part, tile), BF16),
            pltpu.SemaphoreType.DMA((slot_count,)),
        ],
        compiler_params=params(20),
        cost_estimate=cost(0.01),
        name="context_products",
    )(index, tiles, *blocks, *deps)


def turn_back(pieces, start, blocks, scale, pinned=False, deps=()):
    _, _, tile = pieces[0][0].shape
    terms = [term for piece in pieces for term in piece]
    width = sum(piece[0].shape[1] for piece in pieces)
    step = math.gcd(blocks, 8)

    def kernel(start_ref, *refs):
        out_ref, reads = refs[-1], list(refs[: len(terms)])
        for n in range(step):
            columns, at = [], 0
            for piece in pieces:
                columns.append(sum(ref[n].astype(F32) for ref in reads[at : at + len(piece)]))
                at += len(piece)
            out_ref[n * tile : (n + 1) * tile, :] = jnp.concatenate(columns, axis=0).T * scale

    return pl.pallas_call(
        kernel,
        grid_spec=pltpu.PrefetchScalarGridSpec(
            num_scalar_prefetch=1,
            grid=(blocks // step,),
            in_specs=[
                pl.BlockSpec((step, term.shape[1], tile), lambda n, at: (at[0] + n, 0, 0))
                for term in terms
            ]
            + [ANY] * len(deps),
            out_specs=pl.BlockSpec((step * tile, width), lambda n, at: (n, 0)),
        ),
        out_shape=jax.ShapeDtypeStruct((blocks * tile, width), F32),
        compiler_params=params(32),
        cost_estimate=cost(0.01),
        name="turn_back",
    )(start // step, *[in_hbm(term) if pinned else term for term in terms], *deps)


def shards(n_row, n_col, tile_counts, tile_rows, tile_cols, panel):
    counts, rows, cols = tile_counts[0, 0], tile_rows[0, 0], tile_cols[0, 0]
    tile = counts.shape[-1]
    share = panel.shape[0] // tile
    band_rows, band_cols = share * n_col, share * n_row
    chips, bits = n_col // 2, n_row.bit_length() - 1
    block_rows = 2 * share
    my_row, my_col = lax.axis_index("row"), lax.axis_index("col")
    chip, core = my_col // 2, my_col % 2

    def row_swap(x, step):
        pairs = []
        for r in range(n_row):
            for c in range(n_col):
                bit = step if c % 2 == 0 else bits - 1 - step
                pairs.append((r * n_col + c, (r ^ (1 << bit)) * n_col + c))
        return lax.ppermute(x, ("row", "col"), pairs)

    def core_swap(x, keep=lambda c, z: True):
        return lax.ppermute(
            x, "col", [(i, i ^ 1) for i in range(n_col) if keep(i % 2, i // 2)]
        )

    def along(x):
        pairs = []
        for z in range(chips - 1):
            pairs.append((2 * z, 2 * z + 2))
            pairs.append((2 * (chips - 1 - z) + 1, 2 * (chips - 2 - z) + 1))
        return lax.ppermute(x, "col", pairs)

    def row_xor(x, mask):
        return lax.ppermute(x, "row", [(r, r ^ mask) for r in range(n_row)])

    def chip_xor(x, mask):
        return lax.ppermute(x, "col", [(c, c ^ (2 * mask)) for c in range(n_col)])

    sign = jnp.where(core == 0, 1, -1)
    slot_chip = (jnp.arange(2 * chips - 1, dtype=jnp.int32) - (chips - 1)) * sign + chip
    differ = (cols // share) ^ my_row
    turned = sum(((differ >> b) & 1) << (bits - 1 - b) for b in range(bits))
    col_place = jnp.where(core == 0, turned, differ) * share + cols % share
    index = jnp.concatenate([rows, cols, col_place, slot_chip])
    behind = jnp.where(core == 0, chip, chips - 1 - chip).reshape(1)

    def spread(block):
        return {0: block} | {1 << (bits - 1 - step): row_swap(block, step) for step in range(bits)}

    def spread_on(blocks, deps=None):
        blocks = dict(blocks)
        for step in range(1, bits):
            bit = 1 << (bits - 1 - step)
            for at in sorted(blocks):
                if at & -at > bit:
                    block = blocks[at]
                    if deps is not None:
                        shape = block.shape
                        (block,) = add_up([(block, (0, 0))], *shape[:2], [BF16], deps)
                    blocks[at | bit] = row_swap(block, step)
        return [blocks[at] for at in range(n_row)]

    turned_panel = turn_panel(panel, tile, 0, ())
    panel_blocks = spread_on(spread(turned_panel))

    word_part, context = count_sums(counts, rows, cols, band_rows, band_cols, (turned_panel,))
    contexts = [context] + [row_xor(context, mask) for mask in range(1, n_row)]
    power, context_log = smoothed(contexts)
    next_blocks = spread(turn_panel(panel, tile, 1, (power,)))
    half = band_rows // 2
    first, second = word_part[:half], word_part[half:]
    totals = jnp.where(core == 0, first, second) + core_swap(jnp.where(core == 0, second, first))
    for step in range(chips.bit_length() - 1):
        totals = totals + chip_xor(totals, 1 << step)
    other_half = core_swap(totals)
    halves = [jnp.where(core == 0, totals, other_half), jnp.where(core == 0, other_half, totals)]
    power = power + core_swap(power)
    powers = [power] + [chip_xor(power, mask) for mask in range(1, chips)]

    part = panel.shape[1] // (GROUPS * PARTS)
    groups = [None] * GROUPS
    near = [[{} for _ in range(PARTS)] for _ in range(GROUPS)]
    swapped = [[{} for _ in range(PARTS)] for _ in range(GROUPS)]
    own = [[None] * PARTS for _ in range(GROUPS)]
    word_pieces, context_pieces = [], []
    stages = [[[] for _ in range(PARTS)] for _ in range(GROUPS)]
    source = (counts, halves, powers, context_log)
    tiles, *groups[0] = word_products(index, panel_blocks, chips, block_rows, source=source)
    got, passed = [None] * PARTS, {}
    last = ()

    def contexts_of(group, deps):
        for n in range(PARTS):
            blocks = [near[group][n][d] for d in range(chips - 1, 0, -1)] + [own[group][n]]
            blocks += [swapped[group][n][d] for d in range(1, chips)]
            send, keep = context_products(index, tiles, blocks, band_cols, deps)
            deps = (send,)
            stages[group][n].append(send)
            terms, count = [(keep, 0)], band_cols // 2
            for step in range(bits):
                terms.append((row_swap(send, step), 0))
                stages[group][n].append(terms[-1][0])
                if step < bits - 1:
                    count //= 2
                    (send,) = add_up([(x, (2 * y + 1, 0)) for x, y in terms], count, part, [BF16])
                    terms = [(x, 2 * y) for x, y in terms]
            context_pieces.append([x for x, _ in terms])

    for slot in range(chips * GROUPS + chips - 2):
        group, step = slot // chips, slot % chips + 1
        before, hop = group - 1, step + 1
        if group < GROUPS and step < chips:
            given, mine, kept = groups[group]
            if step == 1:
                both = [(mine, (0, 0)), (core_swap(mine), (0, 0))]
            if step == 2:
                (mine_sum,) = add_up(both, block_rows, part * PARTS, [F32], last)
            far = chips - step
            passed[far] = core_swap(
                given[far], lambda c, z, far=far: z >= far if c == 0 else z < chips - far
            )
        for n in range(PARTS):
            if group < GROUPS and step == chips:
                if group:
                    last = (*last, stages[before][n][0])
                terms = [(got[n], (0, 0)), (core_swap(got[n]), (0, 0)), (mine_sum, (0, n))]
                payload, whole = add_up(terms, block_rows, part, [BF16, F32], last)
                own[group][n] = payload
                word_pieces.append([whole])
            elif group < GROUPS:
                terms = [(kept[far], (0, n)), (passed[far], (0, n))]
                if step > 1:
                    terms.append((got[n], (0, 0)))
                other = None
                if group > 0 and hop < chips:
                    other = (near[before][n][hop - 1], behind, step)
                (payload,) = add_up(terms, block_rows, part, [BF16], last, other)
            else:
                payload = near[before][n][hop - 1]
                if GROUPS > 1:
                    last = (*last, stages[before - 1][n][min(step, bits)])
                (payload,) = add_up([(payload, (0, 0))], block_rows, part, [BF16], last)
            got[n] = along(payload)
            last = (payload,)
            if group < GROUPS and step == chips:
                arrived = (group, 1)
            elif group > 0 and hop < chips:
                arrived = (before, hop)
            else:
                continue
            near[arrived[0]][n][arrived[1]] = got[n]
            swapped[arrived[0]][n][arrived[1]] = core_swap(got[n])
        if step == 1 and group < GROUPS - 1:
            panel_blocks = spread_on(next_blocks, last)
        if step == 2 and group < GROUPS - 1:
            _, *groups[group + 1] = word_products(
                index, panel_blocks, chips, block_rows, tiles=tiles, deps=last
            )
            last = (*last, groups[group + 1][0][1])
            if group + 2 < GROUPS:
                next_blocks = spread(turn_panel(panel, tile, group + 2, last))
        if group > 0 and step == chips - 1 and group < GROUPS:
            contexts_of(before, last)
        if group == GROUPS and hop == chips - 1:
            contexts_of(before, ())
    deps = (stages[-1][-1][0],)
    word_out = turn_back(word_pieces, (core * share).reshape(1), share, 1.0, True, deps)
    zero = jnp.zeros((1,), jnp.int32)
    return word_out, turn_back(context_pieces, zero, share, 1.0 / tile)


def solution(mesh):
    in_specs = (
        P("row", "col", None, None, None),
        P("row", "col", None),
        P("row", "col", None),
        P(("col", "row"), None),
    )
    out_specs = (P(("row", "col"), None), P(("col", "row"), None))
    body = functools.partial(shards, mesh.shape["row"], mesh.shape["col"])
    return jax.shard_map(body, mesh=mesh, in_specs=in_specs, out_specs=out_specs, check_vma=False)
```

```python
import functools
import math

import jax
import jax.numpy as jnp
from jax import lax
from jax.experimental import pallas as pl
from jax.experimental.pallas import tpu as pltpu
from jax.sharding import PartitionSpec as P

NEG_SAMPLES = 15
GROUPS = 2
PARTS = 2
F32 = jnp.float32
BF16 = jnp.bfloat16

ANY = pl.BlockSpec(memory_space=pl.ANY)
HBM = pl.BlockSpec(memory_space=pltpu.HBM)
IN_VMEM = pl.BlockSpec(memory_space=pltpu.VMEM)
IN_SMEM = pl.BlockSpec(memory_space=pltpu.SMEM)


def params(mib):
    return pltpu.CompilerParams(vmem_limit_bytes=mib * 2**20)


def cost(microseconds):
    return pl.CostEstimate(flops=0, bytes_accessed=int(microseconds * 3.69e6), transcendentals=0)


def in_hbm(x):
    return pltpu.with_memory_space_constraint(x, pltpu.HBM)


def over_tiles(slots, unroll, first, second):
    unroll = math.gcd(slots, unroll)

    def body(at, carry):
        found = [first(at * unroll + n) for n in range(unroll)]
        for n, one in enumerate(found):
            second(at * unroll + n, one)
        return carry

    lax.fori_loop(0, slots // unroll, body, 0)


def count_sums(counts, rows, cols, band_rows, band_cols, deps):
    slots, tile, _ = counts.shape
    pieces = math.gcd(slots, 10)
    piece = slots // pieces

    def kernel(counts_ref, rows_hbm, cols_hbm, *refs):
        word_ref, context_ref, held, rows_ref, cols_ref, sems = refs[len(deps) :]
        lists = [
            pltpu.make_async_copy(rows_hbm, rows_ref, sems.at[pieces]),
            pltpu.make_async_copy(cols_hbm, cols_ref, sems.at[pieces + 1]),
        ]

        def arriving(n):
            part = pl.ds(n * piece, piece)
            return pltpu.make_async_copy(counts_ref.at[part], held.at[part], sems.at[n])

        for copy in lists + [arriving(n) for n in range(pieces)]:
            copy.start()
        word_ref[...] = jnp.zeros_like(word_ref)
        context_ref[...] = jnp.zeros_like(context_ref)
        for copy in lists:
            copy.wait()

        def sums(n):
            values = held[n].astype(F32)
            return (
                jnp.sum(jnp.sum(values.T.reshape(tile // 8, 8, tile), axis=0), axis=0, keepdims=True),
                jnp.sum(jnp.sum(values.reshape(tile // 8, 8, tile), axis=0), axis=0, keepdims=True),
            )

        def add(n, found):
            word_ref[pl.ds(rows_ref[n], 1), :] += found[0]
            context_ref[pl.ds(cols_ref[n], 1), :] += found[1]

        def one_piece(at, carry):
            arriving(at).wait()
            over_tiles(
                piece, 16, lambda n: sums(at * piece + n), lambda n, found: add(at * piece + n, found)
            )
            return carry

        lax.fori_loop(0, pieces, one_piece, 0)

    return pl.pallas_call(
        kernel,
        in_specs=[HBM] * 3 + [ANY] * len(deps),
        out_specs=[IN_VMEM] * 2,
        out_shape=[
            jax.ShapeDtypeStruct((band_rows, tile), F32),
            jax.ShapeDtypeStruct((band_cols, tile), F32),
        ],
        scratch_shapes=[
            pltpu.VMEM(counts.shape, counts.dtype),
            pltpu.SMEM((slots,), jnp.int32),
            pltpu.SMEM((slots,), jnp.int32),
            pltpu.SemaphoreType.DMA((pieces + 2,)),
        ],
        compiler_params=params(48),
        cost_estimate=cost(0.01),
        name="count_sums",
    )(in_hbm(counts), in_hbm(rows), in_hbm(cols), *deps)


def bundles(core, word_part, contexts):
    band_rows, tile = word_part.shape
    band_cols = contexts[0].shape[0]
    half = band_rows // 2

    def kernel(core_ref, word_ref, *refs):
        keep_ref, give_ref, log_ref = refs[len(contexts) :]
        total = refs[0][...]
        for ref in refs[1 : len(contexts)]:
            total = total + ref[...]
        root = jnp.sqrt(total)
        powers = root * jnp.sqrt(root)
        power = jnp.sum(powers.reshape(band_cols // 8, 8, tile), axis=0)
        for ref, at in ((keep_ref, core_ref[0]), (give_ref, 1 - core_ref[0])):
            ref[:half] = word_ref[pl.ds(pl.multiple_of(at * half, half), half), :]
            ref[half:] = power
        log_ref[...] = jnp.maximum(0.75 * jnp.log(total), 0.0)

    return pl.pallas_call(
        kernel,
        in_specs=[IN_SMEM] + [IN_VMEM] * (1 + len(contexts)),
        out_specs=[IN_VMEM] * 3,
        out_shape=[
            jax.ShapeDtypeStruct((half + 8, tile), F32),
            jax.ShapeDtypeStruct((half + 8, tile), F32),
            jax.ShapeDtypeStruct((band_cols, tile), F32),
        ],
        compiler_params=params(16),
        name="bundles",
    )(core, word_part, *contexts)


def plus(a, b):
    def kernel(a_ref, b_ref, out_ref):
        out_ref[...] = a_ref[...] + b_ref[...]

    return pl.pallas_call(
        kernel,
        in_specs=[IN_VMEM] * 2,
        out_specs=IN_VMEM,
        out_shape=jax.ShapeDtypeStruct(a.shape, a.dtype),
        compiler_params=params(16),
        name="plus",
    )(a, b)


def turn_panel(panel, tile, group, deps):
    blocks, width = panel.shape[0] // tile, panel.shape[1]
    part = width // GROUPS

    def kernel(in_ref, *refs):
        out_ref = refs[-1]
        for n in range(blocks):
            turned = in_ref[n * tile : (n + 1) * tile, :].astype(F32).T.astype(BF16)
            out_ref[n] = turned[group * part : (group + 1) * part]

    return pl.pallas_call(
        kernel,
        in_specs=[IN_VMEM] + [ANY] * len(deps),
        out_specs=IN_VMEM,
        out_shape=jax.ShapeDtypeStruct((blocks, part, tile), BF16),
        compiler_params=params(16),
        name="turn_panel",
    )(in_hbm(panel), *deps)


def add_up(terms, count, width, dtypes, deps=(), other=None):
    tile = terms[0][0].shape[-1]
    n_terms = len(terms)

    def kernel(place_ref, *refs):
        outs = refs[n_terms + (other is not None) + len(deps) :]

        def write():
            total = refs[0][...].astype(F32)
            for ref in refs[1:n_terms]:
                total = total + ref[...].astype(F32)
            for out in outs:
                out[...] = total.astype(out.dtype)

        if other is None:
            write()
        else:
            pl.when(place_ref[0] < other[2])(write)

            @pl.when(place_ref[0] >= other[2])
            def _():
                outs[0][...] = refs[n_terms][...]

    shape = (count, width, tile)
    blocks = [pl.BlockSpec(shape, lambda n, _, at=at: (*at, 0)) for _, at in terms]
    arrays = [array for array, _ in terms]
    if other is None:
        place = jnp.zeros((1,), jnp.int32)
    else:
        place = other[1]
        blocks.append(pl.BlockSpec(shape, lambda n, _: (0, 0, 0)))
        arrays.append(other[0])
    return pl.pallas_call(
        kernel,
        grid_spec=pltpu.PrefetchScalarGridSpec(
            num_scalar_prefetch=1,
            grid=(1,),
            in_specs=blocks + [ANY] * len(deps),
            out_specs=[pl.BlockSpec(shape, lambda n, _: (0, 0, 0))] * len(dtypes),
        ),
        out_shape=[
            (pltpu.HBM if len(dtypes) > 1 and dtype == F32 else jax.ShapeDtypeStruct)(shape, dtype)
            for dtype in dtypes
        ],
        compiler_params=params(24),
        cost_estimate=cost(0.01),
        name="add_up",
    )(place, *arrays, *deps)


def word_products(index, blocks, chips, block_rows, tiles=None, source=None, deps=()):
    shape = (tiles if source is None else source[0]).shape
    slots, tile, _ = shape
    share, width, _ = blocks[0].shape
    slot_count = 2 * chips - 1
    n_in = len(blocks)
    chip_list = 3 * slots
    pieces = math.gcd(slots, 10)
    piece = slots // pieces

    def kernel(index_ref, *refs):
        if source is None:
            tiles_ref, *refs = refs
        else:
            counts_hbm, core_ref, own_ref, other_ref, log_ref, *refs = refs
        block_refs, refs = refs[:n_in], refs[n_in + len(deps) :]
        if source is not None:
            tiles_ref, *refs = refs
        outs, refs = refs[:slot_count], refs[slot_count:]
        acc, band, sems, *refs = refs
        copies = [
            pltpu.make_async_copy(ref, band.at[pl.ds(n * share, share)], sems.at[n])
            for n, ref in enumerate(block_refs)
        ]
        for copy in copies:
            copy.start()
        acc[...] = jnp.zeros_like(acc)
        if source is not None:
            word_log, shift, counts_ref, count_sems = refs

            def arriving(n):
                part = pl.ds(n * piece, piece)
                return pltpu.make_async_copy(
                    counts_hbm.at[part], counts_ref.at[part], count_sems.at[n]
                )

            for n in range(pieces):
                arriving(n).start()
            half = own_ref.shape[0] - 8
            for ref, at in ((own_ref, core_ref[0]), (other_ref, 1 - core_ref[0])):
                rows = pl.ds(pl.multiple_of(at * half, half), half)
                word_log[rows, :] = jnp.log(jnp.maximum(ref[:half], 1.0))
            power = own_ref[half:]
            power = jnp.sum(jnp.sum(power, axis=0, keepdims=True), axis=1, keepdims=True)
            shift[...] = (jnp.log(power) - math.log(NEG_SAMPLES)) - log_ref[...]
        for copy in copies:
            copy.wait()

        def product(n):
            if source is None:
                made = tiles_ref[n]
            else:
                word = word_log[pl.ds(index_ref[n], 1), :]
                word = jnp.broadcast_to(word, (tile, tile)).T
                context = shift[pl.ds(index_ref[slots + n], 1), :]
                pointwise = jnp.log(counts_ref[n].astype(F32)) + (context - word)
                made = jnp.maximum(pointwise, 0.0).astype(BF16)
                tiles_ref[n] = made
            return lax.dot_general(
                band[index_ref[2 * slots + n]],
                made,
                (((1,), (1,)), ((), ())),
                preferred_element_type=F32,
            )

        def add(n, found):
            acc[index_ref[n]] += found

        def one_piece(at, carry):
            if source is not None:
                arriving(at).wait()
            over_tiles(
                piece,
                16,
                lambda n: product(at * piece + n),
                lambda n, found: add(at * piece + n, found),
            )
            return carry

        lax.fori_loop(0, pieces, one_piece, 0)
        for slot, out in enumerate(outs):

            at = index_ref[chip_list + slot]

            @pl.when((at >= 0) & (at < chips))
            def _():
                out[...] = acc[pl.ds(at * block_rows, block_rows)].astype(out.dtype)

    out_shape = [
        pltpu.VMEM((block_rows, width, tile), BF16)
        for slot in range(slot_count)
    ]
    out_specs = [IN_VMEM] * slot_count
    scratch = [
        pltpu.VMEM((chips * block_rows, width, tile), F32),
        pltpu.VMEM((n_in * share, width, tile), BF16),
        pltpu.SemaphoreType.DMA((n_in,)),
    ]
    if source is None:
        operands, operand_specs = [tiles], [IN_VMEM]
    else:
        operands = [in_hbm(source[0]), *source[1:]]
        operand_specs = [HBM, IN_SMEM] + [IN_VMEM] * 3
    if source is not None:
        out_shape = [pltpu.VMEM(shape, BF16)] + out_shape
        out_specs = [IN_VMEM] + out_specs
        scratch += [
            pltpu.VMEM((chips * block_rows, tile), F32),
            pltpu.VMEM(source[-1].shape, F32),
            pltpu.VMEM(shape, jnp.int32),
            pltpu.SemaphoreType.DMA((pieces,)),
        ]
    outs = pl.pallas_call(
        kernel,
        in_specs=[IN_SMEM] + operand_specs + [ANY] * (n_in + len(deps)),
        out_specs=out_specs,
        out_shape=out_shape,
        scratch_shapes=scratch,
        compiler_params=params(40 if source is not None else 32),
        cost_estimate=cost(0.01),
        name="word_products" if source is None else "ppmi_word_products",
    )(index, *operands, *blocks, *deps)
    if source is not None:
        tiles, *outs = outs
    given = {distance: outs[chips - 1 - distance] for distance in range(1, chips)}
    kept = {distance: outs[chips - 1 + distance] for distance in range(1, chips)}
    return tiles, given, outs[chips - 1], kept


def context_products(index, tiles, blocks, band_cols, deps):
    slots, tile, _ = tiles.shape
    block_rows, part, _ = blocks[0].shape
    slot_count = len(blocks)
    chips = (slot_count + 1) // 2
    half = band_cols // 2
    chip_list = 3 * slots

    def kernel(index_ref, tiles_ref, *refs):
        block_refs, refs = refs[:slot_count], refs[slot_count + len(deps) :]
        send, keep, acc, band, sems = refs

        def each_copy(act):
            for slot in range(slot_count):
                at = index_ref[chip_list + slot]

                @pl.when((at >= 0) & (at < chips))
                def _():
                    rows = pl.ds(at * block_rows, block_rows)
                    act(pltpu.make_async_copy(block_refs[slot], band.at[rows], sems.at[slot]))

        each_copy(lambda copy: copy.start())
        acc[...] = jnp.zeros_like(acc)
        each_copy(lambda copy: copy.wait())

        def product(n):
            return jnp.dot(band[index_ref[n]], tiles_ref[n], preferred_element_type=F32)

        def add(n, found):
            acc[index_ref[2 * slots + n]] += found

        over_tiles(slots, 16, product, add)
        send[...] = acc[half:].astype(BF16)
        keep[...] = acc[:half]

    shape = (half, part, tile)
    return pl.pallas_call(
        kernel,
        in_specs=[IN_SMEM, IN_VMEM] + [ANY] * (slot_count + len(deps)),
        out_specs=[IN_VMEM] * 2,
        out_shape=[jax.ShapeDtypeStruct(shape, BF16), jax.ShapeDtypeStruct(shape, F32)],
        scratch_shapes=[
            pltpu.VMEM((band_cols, part, tile), F32),
            pltpu.VMEM((chips * block_rows, part, tile), BF16),
            pltpu.SemaphoreType.DMA((slot_count,)),
        ],
        compiler_params=params(20),
        cost_estimate=cost(0.01),
        name="context_products",
    )(index, tiles, *blocks, *deps)


def turn_back(pieces, start, blocks, scale, pinned=False, deps=()):
    _, _, tile = pieces[0][0].shape
    terms = [term for piece in pieces for term in piece]
    width = sum(piece[0].shape[1] for piece in pieces)
    step = math.gcd(blocks, 8)

    def kernel(start_ref, *refs):
        out_ref, reads = refs[-1], list(refs[: len(terms)])
        for n in range(step):
            columns, at = [], 0
            for piece in pieces:
                columns.append(sum(ref[n].astype(F32) for ref in reads[at : at + len(piece)]))
                at += len(piece)
            out_ref[n * tile : (n + 1) * tile, :] = jnp.concatenate(columns, axis=0).T * scale

    return pl.pallas_call(
        kernel,
        grid_spec=pltpu.PrefetchScalarGridSpec(
            num_scalar_prefetch=1,
            grid=(blocks // step,),
            in_specs=[
                pl.BlockSpec((step, term.shape[1], tile), lambda n, at: (at[0] + n, 0, 0))
                for term in terms
            ]
            + [ANY] * len(deps),
            out_specs=pl.BlockSpec((step * tile, width), lambda n, at: (n, 0)),
        ),
        out_shape=jax.ShapeDtypeStruct((blocks * tile, width), F32),
        compiler_params=params(32),
        cost_estimate=cost(0.01),
        name="turn_back",
    )(start // step, *[in_hbm(term) if pinned else term for term in terms], *deps)


def shards(n_row, n_col, tile_counts, tile_rows, tile_cols, panel):
    counts, rows, cols = tile_counts[0, 0], tile_rows[0, 0], tile_cols[0, 0]
    tile = counts.shape[-1]
    share = panel.shape[0] // tile
    band_rows, band_cols = share * n_col, share * n_row
    chips, bits = n_col // 2, n_row.bit_length() - 1
    block_rows = 2 * share
    my_row, my_col = lax.axis_index("row"), lax.axis_index("col")
    chip, core = my_col // 2, my_col % 2

    def row_swap(x, step):
        pairs = []
        for r in range(n_row):
            for c in range(n_col):
                bit = step if c % 2 == 0 else bits - 1 - step
                pairs.append((r * n_col + c, (r ^ (1 << bit)) * n_col + c))
        return lax.ppermute(x, ("row", "col"), pairs)

    def core_swap(x, keep=lambda c, z: True):
        return lax.ppermute(
            x, "col", [(i, i ^ 1) for i in range(n_col) if keep(i % 2, i // 2)]
        )

    def along(x):
        pairs = []
        for z in range(chips - 1):
            pairs.append((2 * z, 2 * z + 2))
            pairs.append((2 * (chips - 1 - z) + 1, 2 * (chips - 2 - z) + 1))
        return lax.ppermute(x, "col", pairs)

    def row_xor(x, mask):
        return lax.ppermute(x, "row", [(r, r ^ mask) for r in range(n_row)])

    def chip_xor(x, mask):
        return lax.ppermute(x, "col", [(c, c ^ (2 * mask)) for c in range(n_col)])

    sign = jnp.where(core == 0, 1, -1)
    slot_chip = (jnp.arange(2 * chips - 1, dtype=jnp.int32) - (chips - 1)) * sign + chip
    differ = (cols // share) ^ my_row
    turned = sum(((differ >> b) & 1) << (bits - 1 - b) for b in range(bits))
    col_place = jnp.where(core == 0, turned, differ) * share + cols % share
    index = jnp.concatenate([rows, cols, col_place, slot_chip])
    behind = jnp.where(core == 0, chip, chips - 1 - chip).reshape(1)

    def spread(block):
        return {0: block} | {1 << (bits - 1 - step): row_swap(block, step) for step in range(bits)}

    def spread_on(blocks, deps=None):
        blocks = dict(blocks)
        for step in range(1, bits):
            bit = 1 << (bits - 1 - step)
            for at in sorted(blocks):
                if at & -at > bit:
                    block = blocks[at]
                    if deps is not None:
                        shape = block.shape
                        (block,) = add_up([(block, (0, 0))], *shape[:2], [BF16], deps)
                    blocks[at | bit] = row_swap(block, step)
        return [blocks[at] for at in range(n_row)]

    turned_panel = turn_panel(panel, tile, 0, ())
    panel_blocks = spread_on(spread(turned_panel))

    word_part, context = count_sums(counts, rows, cols, band_rows, band_cols, (turned_panel,))
    contexts = [context] + [row_xor(context, mask) for mask in range(1, n_row)]
    this_core = core.reshape(1)
    bundle, given, context_log = bundles(this_core, word_part, contexts)
    next_blocks = spread(turn_panel(panel, tile, 1, (bundle,)))
    bundle = plus(bundle, core_swap(given))
    for step in range(chips.bit_length() - 1):
        bundle = plus(bundle, chip_xor(bundle, 1 << step))

    part = panel.shape[1] // (GROUPS * PARTS)
    groups = [None] * GROUPS
    near = [[{} for _ in range(PARTS)] for _ in range(GROUPS)]
    swapped = [[{} for _ in range(PARTS)] for _ in range(GROUPS)]
    own = [[None] * PARTS for _ in range(GROUPS)]
    word_pieces, context_pieces = [], []
    stages = [[[] for _ in range(PARTS)] for _ in range(GROUPS)]
    source = (counts, this_core, bundle, core_swap(bundle), context_log)
    tiles, *groups[0] = word_products(index, panel_blocks, chips, block_rows, source=source)
    got, passed = [None] * PARTS, {}
    last = ()

    def contexts_of(group, n, deps):
        blocks = [near[group][n][d] for d in range(chips - 1, 0, -1)] + [own[group][n]]
        blocks += [swapped[group][n][d] for d in range(1, chips)]
        send, keep = context_products(index, tiles, blocks, band_cols, deps)
        stages[group][n].append(send)
        terms, count = [(keep, 0)], band_cols // 2
        for step in range(bits):
            terms.append((row_swap(send, step), 0))
            stages[group][n].append(terms[-1][0])
            if step < bits - 1:
                count //= 2
                (send,) = add_up([(x, (2 * y + 1, 0)) for x, y in terms], count, part, [BF16])
                terms = [(x, 2 * y) for x, y in terms]
        context_pieces.append([x for x, _ in terms])

    for slot in range(chips * GROUPS + chips - 2):
        group, step = slot // chips, slot % chips + 1
        before, hop = group - 1, step + 1
        if group < GROUPS and step < chips:
            given, mine, kept = groups[group]
            if step == 1:
                both = [(mine, (0, 0)), (core_swap(mine), (0, 0))]
            if step == 2:
                (mine_sum,) = add_up(both, block_rows, part * PARTS, [F32], last)
            far = chips - step
            passed[far] = core_swap(
                given[far], lambda c, z, far=far: z >= far if c == 0 else z < chips - far
            )
        for n in range(PARTS):
            if group < GROUPS and step == chips:
                if group:
                    last = (*last, stages[before][n][0])
                    if n:
                        (got[n],) = add_up([(got[n], (0, 0))], block_rows, part, [BF16], first_sent)
                terms = [(got[n], (0, 0)), (core_swap(got[n]), (0, 0)), (mine_sum, (0, n))]
                payload, whole = add_up(terms, block_rows, part, [BF16, F32], last)
                own[group][n] = payload
                if group and n + 1 < PARTS:
                    contexts_of(before, n + 1, (payload,))
                word_pieces.append([whole])
            elif group < GROUPS:
                terms = [(kept[far], (0, n)), (passed[far], (0, n))]
                if step > 1:
                    terms.append((got[n], (0, 0)))
                other = None
                if group > 0 and hop < chips:
                    other = (near[before][n][hop - 1], behind, step)
                (payload,) = add_up(terms, block_rows, part, [BF16], last, other)
            else:
                payload = near[before][n][hop - 1]
                if GROUPS > 1:
                    last = (*last, stages[before - 1][n][min(step, bits)])
                (payload,) = add_up([(payload, (0, 0))], block_rows, part, [BF16], last)
            got[n] = along(payload)
            last = (payload,)
            if group < GROUPS and step == chips:
                arrived = (group, 1)
            elif group > 0 and hop < chips:
                arrived = (before, hop)
            else:
                continue
            if group == GROUPS and hop == chips - 1 and n > 0:
                gate = stages[before][n - 1][:1]
                (got[n],) = add_up([(got[n], (0, 0))], block_rows, part, [BF16], gate)
            near[arrived[0]][n][arrived[1]] = got[n]
            swapped[arrived[0]][n][arrived[1]] = core_swap(got[n])
            if group == GROUPS and hop == chips - 1:
                contexts_of(before, n, ())
        if step == 1 and group < GROUPS - 1:
            panel_blocks = spread_on(next_blocks, last)
        if step == 2 and group < GROUPS - 1:
            _, *groups[group + 1] = word_products(
                index, panel_blocks, chips, block_rows, tiles=tiles, deps=last
            )
            last = (*last, groups[group + 1][0][1])
            if group + 2 < GROUPS:
                next_blocks = spread(turn_panel(panel, tile, group + 2, last))
        if group > 0 and step == chips - 1 and group < GROUPS:
            contexts_of(before, 0, last)
            first_sent = stages[before][0][:1]
    deps = (stages[-1][-1][0],)
    word_out = turn_back(word_pieces, (core * share).reshape(1), share, 1.0, True, deps)
    zero = jnp.zeros((1,), jnp.int32)
    return word_out, turn_back(context_pieces, zero, share, 1.0 / tile)


def solution(mesh):
    in_specs = (
        P("row", "col", None, None, None),
        P("row", "col", None),
        P("row", "col", None),
        P(("col", "row"), None),
    )
    out_specs = (P(("row", "col"), None), P(("col", "row"), None))
    body = functools.partial(shards, mesh.shape["row"], mesh.shape["col"])
    return jax.shard_map(body, mesh=mesh, in_specs=in_specs, out_specs=out_specs, check_vma=False)
```

```python
import functools
import math

import jax
import jax.numpy as jnp
from jax import lax
from jax.experimental import pallas as pl
from jax.experimental.pallas import tpu as pltpu
from jax.sharding import PartitionSpec as P

NEG_SAMPLES = 15
GROUPS = 2
PARTS = 2
F32 = jnp.float32
BF16 = jnp.bfloat16

ANY = pl.BlockSpec(memory_space=pl.ANY)
HBM = pl.BlockSpec(memory_space=pltpu.HBM)
IN_VMEM = pl.BlockSpec(memory_space=pltpu.VMEM)
IN_SMEM = pl.BlockSpec(memory_space=pltpu.SMEM)


def params(mib):
    return pltpu.CompilerParams(vmem_limit_bytes=mib * 2**20)


def cost(microseconds):
    return pl.CostEstimate(flops=0, bytes_accessed=int(microseconds * 3.69e6), transcendentals=0)


def in_hbm(x):
    return pltpu.with_memory_space_constraint(x, pltpu.HBM)


def over_tiles(slots, unroll, first, second):
    unroll = math.gcd(slots, unroll)

    def body(at, carry):
        found = [first(at * unroll + n) for n in range(unroll)]
        for n, one in enumerate(found):
            second(at * unroll + n, one)
        return carry

    lax.fori_loop(0, slots // unroll, body, 0)


def count_sums(counts, rows, cols, band_rows, band_cols, deps):
    slots, tile, _ = counts.shape
    pieces = math.gcd(slots, 10)
    piece = slots // pieces

    def kernel(counts_ref, rows_hbm, cols_hbm, *refs):
        word_ref, context_ref, held, rows_ref, cols_ref, sems = refs[len(deps) :]
        lists = [
            pltpu.make_async_copy(rows_hbm, rows_ref, sems.at[pieces]),
            pltpu.make_async_copy(cols_hbm, cols_ref, sems.at[pieces + 1]),
        ]

        def arriving(n):
            part = pl.ds(n * piece, piece)
            return pltpu.make_async_copy(counts_ref.at[part], held.at[part], sems.at[n])

        for copy in lists + [arriving(n) for n in range(pieces)]:
            copy.start()
        word_ref[...] = jnp.zeros_like(word_ref)
        context_ref[...] = jnp.zeros_like(context_ref)
        for copy in lists:
            copy.wait()

        def sums(n):
            values = held[n].astype(F32)
            return (
                jnp.sum(jnp.sum(values.T.reshape(tile // 8, 8, tile), axis=0), axis=0, keepdims=True),
                jnp.sum(jnp.sum(values.reshape(tile // 8, 8, tile), axis=0), axis=0, keepdims=True),
            )

        def add(n, found):
            word_ref[pl.ds(rows_ref[n], 1), :] += found[0]
            context_ref[pl.ds(cols_ref[n], 1), :] += found[1]

        def one_piece(at, carry):
            arriving(at).wait()
            over_tiles(
                piece, 16, lambda n: sums(at * piece + n), lambda n, found: add(at * piece + n, found)
            )
            return carry

        lax.fori_loop(0, pieces, one_piece, 0)

    return pl.pallas_call(
        kernel,
        in_specs=[HBM] * 3 + [ANY] * len(deps),
        out_specs=[IN_VMEM] * 2,
        out_shape=[
            jax.ShapeDtypeStruct((band_rows, tile), F32),
            jax.ShapeDtypeStruct((band_cols, tile), F32),
        ],
        scratch_shapes=[
            pltpu.VMEM(counts.shape, counts.dtype),
            pltpu.SMEM((slots,), jnp.int32),
            pltpu.SMEM((slots,), jnp.int32),
            pltpu.SemaphoreType.DMA((pieces + 2,)),
        ],
        compiler_params=params(48),
        cost_estimate=cost(0.01),
        name="count_sums",
    )(in_hbm(counts), in_hbm(rows), in_hbm(cols), *deps)


def bundles(core, word_part, contexts):
    band_rows, tile = word_part.shape
    band_cols = contexts[0].shape[0]
    half = band_rows // 2

    def kernel(core_ref, word_ref, *refs):
        keep_ref, give_ref, log_ref = refs[len(contexts) :]
        total = refs[0][...]
        for ref in refs[1 : len(contexts)]:
            total = total + ref[...]
        root = jnp.sqrt(total)
        powers = root * jnp.sqrt(root)
        power = jnp.sum(powers.reshape(band_cols // 8, 8, tile), axis=0)
        for ref, at in ((keep_ref, core_ref[0]), (give_ref, 1 - core_ref[0])):
            ref[:half] = word_ref[pl.ds(pl.multiple_of(at * half, half), half), :]
            ref[half:] = power
        log_ref[...] = jnp.maximum(0.75 * jnp.log(total), 0.0)

    return pl.pallas_call(
        kernel,
        in_specs=[IN_SMEM] + [IN_VMEM] * (1 + len(contexts)),
        out_specs=[IN_VMEM] * 3,
        out_shape=[
            jax.ShapeDtypeStruct((half + 8, tile), F32),
            jax.ShapeDtypeStruct((half + 8, tile), F32),
            jax.ShapeDtypeStruct((band_cols, tile), F32),
        ],
        compiler_params=params(16),
        name="bundles",
    )(core, word_part, *contexts)


def plus(a, b):
    def kernel(a_ref, b_ref, out_ref):
        out_ref[...] = a_ref[...] + b_ref[...]

    return pl.pallas_call(
        kernel,
        in_specs=[IN_VMEM] * 2,
        out_specs=IN_VMEM,
        out_shape=jax.ShapeDtypeStruct(a.shape, a.dtype),
        compiler_params=params(16),
        name="plus",
    )(a, b)


def turn_panel(panel, tile, group, deps):
    blocks, width = panel.shape[0] // tile, panel.shape[1]
    part = width // GROUPS

    def kernel(in_ref, *refs):
        out_ref = refs[-1]
        for n in range(blocks):
            turned = in_ref[n * tile : (n + 1) * tile, :].astype(F32).T.astype(BF16)
            out_ref[n] = turned[group * part : (group + 1) * part]

    return pl.pallas_call(
        kernel,
        in_specs=[IN_VMEM] + [ANY] * len(deps),
        out_specs=IN_VMEM,
        out_shape=jax.ShapeDtypeStruct((blocks, part, tile), BF16),
        compiler_params=params(16),
        name="turn_panel",
    )(in_hbm(panel), *deps)


def add_up(terms, count, width, dtypes, deps=(), other=None):
    tile = terms[0][0].shape[-1]
    n_terms = len(terms)

    def kernel(place_ref, *refs):
        outs = refs[n_terms + (other is not None) + len(deps) :]

        def write():
            total = refs[0][...].astype(F32)
            for ref in refs[1:n_terms]:
                total = total + ref[...].astype(F32)
            for out in outs:
                out[...] = total.astype(out.dtype)

        if other is None:
            write()
        else:
            pl.when(place_ref[0] < other[2])(write)

            @pl.when(place_ref[0] >= other[2])
            def _():
                outs[0][...] = refs[n_terms][...]

    shape = (count, width, tile)
    blocks = [pl.BlockSpec(shape, lambda n, _, at=at: (*at, 0)) for _, at in terms]
    arrays = [array for array, _ in terms]
    if other is None:
        place = jnp.zeros((1,), jnp.int32)
    else:
        place = other[1]
        blocks.append(pl.BlockSpec(shape, lambda n, _: (0, 0, 0)))
        arrays.append(other[0])
    return pl.pallas_call(
        kernel,
        grid_spec=pltpu.PrefetchScalarGridSpec(
            num_scalar_prefetch=1,
            grid=(1,),
            in_specs=blocks + [ANY] * len(deps),
            out_specs=[pl.BlockSpec(shape, lambda n, _: (0, 0, 0))] * len(dtypes),
        ),
        out_shape=[
            (pltpu.HBM if len(dtypes) > 1 and dtype == F32 else jax.ShapeDtypeStruct)(shape, dtype)
            for dtype in dtypes
        ],
        compiler_params=params(24),
        cost_estimate=cost(0.01),
        name="add_up",
    )(place, *arrays, *deps)


def word_products(index, blocks, chips, block_rows, tiles=None, source=None, deps=()):
    shape = (tiles if source is None else source[0]).shape
    slots, tile, _ = shape
    share, width, _ = blocks[0].shape
    slot_count = 2 * chips - 1
    n_in = len(blocks)
    chip_list = 3 * slots
    pieces = math.gcd(slots, 10)
    piece = slots // pieces

    def kernel(index_ref, *refs):
        if source is None:
            tiles_ref, *refs = refs
        else:
            counts_hbm, core_ref, own_ref, other_ref, log_ref, *refs = refs
        block_refs, refs = refs[:n_in], refs[n_in + len(deps) :]
        if source is not None:
            tiles_ref, *refs = refs
        outs, refs = refs[:slot_count], refs[slot_count:]
        acc, band, sems, *refs = refs
        copies = [
            pltpu.make_async_copy(ref, band.at[pl.ds(n * share, share)], sems.at[n])
            for n, ref in enumerate(block_refs)
        ]
        for copy in copies:
            copy.start()
        acc[...] = jnp.zeros_like(acc)
        if source is not None:
            word_log, shift, counts_ref, count_sems = refs

            def arriving(n):
                part = pl.ds(n * piece, piece)
                return pltpu.make_async_copy(
                    counts_hbm.at[part], counts_ref.at[part], count_sems.at[n]
                )

            for n in range(pieces):
                arriving(n).start()
            half = own_ref.shape[0] - 8
            for ref, at in ((own_ref, core_ref[0]), (other_ref, 1 - core_ref[0])):
                rows = pl.ds(pl.multiple_of(at * half, half), half)
                word_log[rows, :] = jnp.log(jnp.maximum(ref[:half], 1.0))
            power = own_ref[half:]
            power = jnp.sum(jnp.sum(power, axis=0, keepdims=True), axis=1, keepdims=True)
            shift[...] = (jnp.log(power) - math.log(NEG_SAMPLES)) - log_ref[...]
        for copy in copies:
            copy.wait()

        def product(n):
            if source is None:
                made = tiles_ref[n]
            else:
                word = word_log[pl.ds(index_ref[n], 1), :]
                word = jnp.broadcast_to(word, (tile, tile)).T
                context = shift[pl.ds(index_ref[slots + n], 1), :]
                pointwise = jnp.log(counts_ref[n].astype(F32)) + (context - word)
                made = jnp.maximum(pointwise, 0.0).astype(BF16)
                tiles_ref[n] = made
            return lax.dot_general(
                band[index_ref[2 * slots + n]],
                made,
                (((1,), (1,)), ((), ())),
                preferred_element_type=F32,
            )

        def add(n, found):
            acc[index_ref[n]] += found

        def one_piece(at, carry):
            if source is not None:
                arriving(at).wait()
            over_tiles(
                piece,
                16,
                lambda n: product(at * piece + n),
                lambda n, found: add(at * piece + n, found),
            )
            return carry

        lax.fori_loop(0, pieces, one_piece, 0)
        for slot, out in enumerate(outs):

            at = index_ref[chip_list + slot]

            @pl.when((at >= 0) & (at < chips))
            def _():
                out[...] = acc[pl.ds(at * block_rows, block_rows)].astype(out.dtype)

    out_shape = [
        pltpu.VMEM((block_rows, width, tile), BF16)
        for slot in range(slot_count)
    ]
    out_specs = [IN_VMEM] * slot_count
    scratch = [
        pltpu.VMEM((chips * block_rows, width, tile), F32),
        pltpu.VMEM((n_in * share, width, tile), BF16),
        pltpu.SemaphoreType.DMA((n_in,)),
    ]
    if source is None:
        operands, operand_specs = [tiles], [IN_VMEM]
    else:
        operands = [in_hbm(source[0]), *source[1:]]
        operand_specs = [HBM, IN_SMEM] + [IN_VMEM] * 3
    if source is not None:
        out_shape = [pltpu.VMEM(shape, BF16)] + out_shape
        out_specs = [IN_VMEM] + out_specs
        scratch += [
            pltpu.VMEM((chips * block_rows, tile), F32),
            pltpu.VMEM(source[-1].shape, F32),
            pltpu.VMEM(shape, jnp.int32),
            pltpu.SemaphoreType.DMA((pieces,)),
        ]
    outs = pl.pallas_call(
        kernel,
        in_specs=[IN_SMEM] + operand_specs + [ANY] * (n_in + len(deps)),
        out_specs=out_specs,
        out_shape=out_shape,
        scratch_shapes=scratch,
        compiler_params=params(40 if source is not None else 32),
        cost_estimate=cost(0.01),
        name="word_products" if source is None else "ppmi_word_products",
    )(index, *operands, *blocks, *deps)
    if source is not None:
        tiles, *outs = outs
    given = {distance: outs[chips - 1 - distance] for distance in range(1, chips)}
    kept = {distance: outs[chips - 1 + distance] for distance in range(1, chips)}
    return tiles, given, outs[chips - 1], kept


def context_products(index, tiles, blocks, band_cols, deps):
    slots, tile, _ = tiles.shape
    block_rows, part, _ = blocks[0][0].shape
    slot_count, parts = len(blocks), len(blocks[0])
    width = part * parts
    chips = (slot_count + 1) // 2
    half = band_cols // 2
    chip_list = 3 * slots

    def kernel(index_ref, tiles_ref, *refs):
        block_refs, refs = refs[: slot_count * parts], refs[slot_count * parts + len(deps) :]
        send, keep, acc, band, sems = refs

        def each_copy(act):
            for slot in range(slot_count):
                at = index_ref[chip_list + slot]

                @pl.when((at >= 0) & (at < chips))
                def _():
                    for n in range(parts):
                        rows, columns = pl.ds(at * block_rows, block_rows), pl.ds(n * part, part)
                        act(
                            pltpu.make_async_copy(
                                block_refs[slot * parts + n], band.at[rows, columns], sems.at[slot, n]
                            )
                        )

        each_copy(lambda copy: copy.start())
        acc[...] = jnp.zeros_like(acc)
        each_copy(lambda copy: copy.wait())

        def product(n):
            return jnp.dot(band[index_ref[n]], tiles_ref[n], preferred_element_type=F32)

        def add(n, found):
            acc[index_ref[2 * slots + n]] += found

        over_tiles(slots, 16, product, add)
        send[...] = acc[half:].astype(BF16)
        keep[...] = acc[:half]

    shape = (half, width, tile)
    return pl.pallas_call(
        kernel,
        in_specs=[IN_SMEM, IN_VMEM] + [ANY] * (slot_count * parts + len(deps)),
        out_specs=[IN_VMEM] * 2,
        out_shape=[jax.ShapeDtypeStruct(shape, BF16), jax.ShapeDtypeStruct(shape, F32)],
        scratch_shapes=[
            pltpu.VMEM((band_cols, width, tile), F32),
            pltpu.VMEM((chips * block_rows, width, tile), BF16),
            pltpu.SemaphoreType.DMA((slot_count, parts)),
        ],
        compiler_params=params(32),
        cost_estimate=cost(0.01),
        name="context_products",
    )(index, tiles, *[ref for block in blocks for ref in block], *deps)


def turn_back(pieces, start, blocks, scale, pinned=False, deps=()):
    _, _, tile = pieces[0][0].shape
    terms = [term for piece in pieces for term in piece]
    width = sum(piece[0].shape[1] for piece in pieces)
    step = math.gcd(blocks, 8)

    def kernel(start_ref, *refs):
        out_ref, reads = refs[-1], list(refs[: len(terms)])
        for n in range(step):
            columns, at = [], 0
            for piece in pieces:
                columns.append(sum(ref[n].astype(F32) for ref in reads[at : at + len(piece)]))
                at += len(piece)
            out_ref[n * tile : (n + 1) * tile, :] = jnp.concatenate(columns, axis=0).T * scale

    return pl.pallas_call(
        kernel,
        grid_spec=pltpu.PrefetchScalarGridSpec(
            num_scalar_prefetch=1,
            grid=(blocks // step,),
            in_specs=[
                pl.BlockSpec((step, term.shape[1], tile), lambda n, at: (at[0] + n, 0, 0))
                for term in terms
            ]
            + [ANY] * len(deps),
            out_specs=pl.BlockSpec((step * tile, width), lambda n, at: (n, 0)),
        ),
        out_shape=jax.ShapeDtypeStruct((blocks * tile, width), F32),
        compiler_params=params(32),
        cost_estimate=cost(0.01),
        name="turn_back",
    )(start // step, *[in_hbm(term) if pinned else term for term in terms], *deps)


def shards(n_row, n_col, tile_counts, tile_rows, tile_cols, panel):
    counts, rows, cols = tile_counts[0, 0], tile_rows[0, 0], tile_cols[0, 0]
    tile = counts.shape[-1]
    share = panel.shape[0] // tile
    band_rows, band_cols = share * n_col, share * n_row
    chips, bits = n_col // 2, n_row.bit_length() - 1
    block_rows = 2 * share
    my_row, my_col = lax.axis_index("row"), lax.axis_index("col")
    chip, core = my_col // 2, my_col % 2

    def row_swap(x, step):
        pairs = []
        for r in range(n_row):
            for c in range(n_col):
                bit = step if c % 2 == 0 else bits - 1 - step
                pairs.append((r * n_col + c, (r ^ (1 << bit)) * n_col + c))
        return lax.ppermute(x, ("row", "col"), pairs)

    def core_swap(x, keep=lambda c, z: True):
        return lax.ppermute(
            x, "col", [(i, i ^ 1) for i in range(n_col) if keep(i % 2, i // 2)]
        )

    def along(x):
        pairs = []
        for z in range(chips - 1):
            pairs.append((2 * z, 2 * z + 2))
            pairs.append((2 * (chips - 1 - z) + 1, 2 * (chips - 2 - z) + 1))
        return lax.ppermute(x, "col", pairs)

    def row_xor(x, mask):
        return lax.ppermute(x, "row", [(r, r ^ mask) for r in range(n_row)])

    def chip_xor(x, mask):
        return lax.ppermute(x, "col", [(c, c ^ (2 * mask)) for c in range(n_col)])

    sign = jnp.where(core == 0, 1, -1)
    slot_chip = (jnp.arange(2 * chips - 1, dtype=jnp.int32) - (chips - 1)) * sign + chip
    differ = (cols // share) ^ my_row
    turned = sum(((differ >> b) & 1) << (bits - 1 - b) for b in range(bits))
    col_place = jnp.where(core == 0, turned, differ) * share + cols % share
    index = jnp.concatenate([rows, cols, col_place, slot_chip])
    behind = jnp.where(core == 0, chip, chips - 1 - chip).reshape(1)

    def spread(block):
        return {0: block} | {1 << (bits - 1 - step): row_swap(block, step) for step in range(bits)}

    def spread_on(blocks, deps=None):
        blocks = dict(blocks)
        for step in range(1, bits):
            bit = 1 << (bits - 1 - step)
            for at in sorted(blocks):
                if at & -at > bit:
                    block = blocks[at]
                    if deps is not None:
                        shape = block.shape
                        (block,) = add_up([(block, (0, 0))], *shape[:2], [BF16], deps)
                    blocks[at | bit] = row_swap(block, step)
        return [blocks[at] for at in range(n_row)]

    turned_panel = turn_panel(panel, tile, 0, ())
    panel_blocks = spread_on(spread(turned_panel))

    word_part, context = count_sums(counts, rows, cols, band_rows, band_cols, (turned_panel,))
    contexts = [context] + [row_xor(context, mask) for mask in range(1, n_row)]
    this_core = core.reshape(1)
    bundle, given, context_log = bundles(this_core, word_part, contexts)
    bundle = plus(bundle, core_swap(given))
    for step in range(chips.bit_length() - 1):
        bundle = plus(bundle, chip_xor(bundle, 1 << step))

    part = panel.shape[1] // (GROUPS * PARTS)
    groups = [None] * GROUPS
    near = [[{} for _ in range(PARTS)] for _ in range(GROUPS)]
    swapped = [[{} for _ in range(PARTS)] for _ in range(GROUPS)]
    own = [[None] * PARTS for _ in range(GROUPS)]
    word_pieces, context_pieces = [], []
    stages, through = [], []
    source = (counts, this_core, bundle, core_swap(bundle), context_log)
    tiles, *groups[0] = word_products(index, panel_blocks, chips, block_rows, source=source)
    got, passed = [None] * PARTS, {}
    last = ()

    def contexts_of(group, parts, deps):
        blocks = [[near[group][n][d] for n in parts] for d in range(chips - 1, 0, -1)]
        blocks.append([own[group][n] for n in parts])
        blocks += [[swapped[group][n][d] for n in parts] for d in range(1, chips)]
        send, keep = context_products(index, tiles, blocks, band_cols, deps)
        sent = [send]
        terms, count = [(keep, 0)], band_cols // 2
        for step in range(bits):
            terms.append((row_swap(send, step), 0))
            sent.append(terms[-1][0])
            if step < bits - 1:
                count //= 2
                (send,) = add_up(
                    [(x, (2 * y + 1, 0)) for x, y in terms], count, part * len(parts), [BF16]
                )
                terms = [(x, 2 * y) for x, y in terms]
        context_pieces.append([x for x, _ in terms])
        return sent

    for slot in range(chips * GROUPS + chips - 2):
        group, step = slot // chips, slot % chips + 1
        before, hop = group - 1, step + 1
        if group < GROUPS and step < chips:
            given, mine, kept = groups[group]
            if step == 1:
                both = [(mine, (0, 0)), (core_swap(mine), (0, 0))]
            if step == 2:
                (mine_sum,) = add_up(both, block_rows, part * PARTS, [F32], last)
            far = chips - step
            passed[far] = core_swap(
                given[far], lambda c, z, far=far: z >= far if c == 0 else z < chips - far
            )
        for n in range(PARTS):
            if group < GROUPS and step == chips:
                terms = [(got[n], (0, 0)), (core_swap(got[n]), (0, 0)), (mine_sum, (0, n))]
                payload, whole = add_up(terms, block_rows, part, [BF16, F32], last)
                own[group][n] = payload
                if group and n == PARTS - 1:
                    through = contexts_of(before, range(PARTS), (payload,))
                word_pieces.append([whole])
            elif group < GROUPS:
                terms = [(kept[far], (0, n)), (passed[far], (0, n))]
                if step > 1:
                    terms.append((got[n], (0, 0)))
                other = None
                if group > 0 and hop < chips:
                    other = (near[before][n][hop - 1], behind, step)
                (payload,) = add_up(terms, block_rows, part, [BF16], last, other)
            else:
                payload = near[before][n][hop - 1]
                if through and n == (0 if step == 1 else PARTS - 1):
                    last = (*last, through[min(step - 1, bits)])
                (payload,) = add_up([(payload, (0, 0))], block_rows, part, [BF16], last)
            got[n] = along(payload)
            last = (payload,)
            if n == 0 and step == 1 and group < GROUPS - 1:
                next_blocks = spread(turn_panel(panel, tile, group + 1, last))
            if group < GROUPS and step == chips:
                arrived = (group, 1)
            elif group > 0 and hop < chips:
                arrived = (before, hop)
            else:
                continue
            if group == GROUPS and hop == chips - 1 and n > 0:
                (got[n],) = add_up([(got[n], (0, 0))], block_rows, part, [BF16], stages[:1])
            near[arrived[0]][n][arrived[1]] = got[n]
            swapped[arrived[0]][n][arrived[1]] = core_swap(got[n])
            if group == GROUPS and hop == chips - 1:
                stages = contexts_of(before, (n,), through[-1:])
        if step == 2 and group < GROUPS - 1:
            panel_blocks = spread_on(next_blocks, last)
        if step == chips - 1 and group < GROUPS - 1:
            _, *groups[group + 1] = word_products(
                index, panel_blocks, chips, block_rows, tiles=tiles, deps=last
            )
            made = (groups[group + 1][0][1],)

    deps = (stages[0],)
    word_out = turn_back(word_pieces, (core * share).reshape(1), share, 1.0, True, deps)
    zero = jnp.zeros((1,), jnp.int32)
    return word_out, turn_back(context_pieces, zero, share, 1.0 / tile)


def solution(mesh):
    in_specs = (
        P("row", "col", None, None, None),
        P("row", "col", None),
        P("row", "col", None),
        P(("col", "row"), None),
    )
    out_specs = (P(("row", "col"), None), P(("col", "row"), None))
    body = functools.partial(shards, mesh.shape["row"], mesh.shape["col"])
    return jax.shard_map(body, mesh=mesh, in_specs=in_specs, out_specs=out_specs, check_vma=False)
```

```python
import functools
import math

import jax
import jax.numpy as jnp
from jax import lax
from jax.experimental import pallas as pl
from jax.experimental.pallas import tpu as pltpu
from jax.sharding import PartitionSpec as P

NEG_SAMPLES = 15
GROUPS = 2
PARTS = 2
F32 = jnp.float32
BF16 = jnp.bfloat16

ANY = pl.BlockSpec(memory_space=pl.ANY)
HBM = pl.BlockSpec(memory_space=pltpu.HBM)
IN_VMEM = pl.BlockSpec(memory_space=pltpu.VMEM)
IN_SMEM = pl.BlockSpec(memory_space=pltpu.SMEM)


def params(mib):
    return pltpu.CompilerParams(vmem_limit_bytes=mib * 2**20)


def cost(microseconds):
    return pl.CostEstimate(flops=0, bytes_accessed=int(microseconds * 3.69e6), transcendentals=0)


def in_hbm(x):
    return pltpu.with_memory_space_constraint(x, pltpu.HBM)


def over_tiles(slots, unroll, first, second):
    unroll = math.gcd(slots, unroll)

    def body(at, carry):
        found = [first(at * unroll + n) for n in range(unroll)]
        for n, one in enumerate(found):
            second(at * unroll + n, one)
        return carry

    lax.fori_loop(0, slots // unroll, body, 0)


def count_sums(counts, rows, cols, band_rows, band_cols, deps):
    slots, tile, _ = counts.shape
    pieces = math.gcd(slots, 5)
    piece = slots // pieces

    def kernel(counts_ref, rows_hbm, cols_hbm, *refs):
        word_ref, context_ref, held, rows_ref, cols_ref, sems = refs[len(deps) :]
        lists = [
            pltpu.make_async_copy(rows_hbm, rows_ref, sems.at[pieces]),
            pltpu.make_async_copy(cols_hbm, cols_ref, sems.at[pieces + 1]),
        ]

        def arriving(n):
            part = pl.ds(n * piece, piece)
            return pltpu.make_async_copy(counts_ref.at[part], held.at[part], sems.at[n])

        for copy in lists + [arriving(n) for n in range(pieces)]:
            copy.start()
        word_ref[...] = jnp.zeros_like(word_ref)
        context_ref[...] = jnp.zeros_like(context_ref)
        for copy in lists:
            copy.wait()

        def sums(n):
            values = held[n].astype(F32)
            return (
                jnp.sum(jnp.sum(values.T.reshape(tile // 8, 8, tile), axis=0), axis=0, keepdims=True),
                jnp.sum(jnp.sum(values.reshape(tile // 8, 8, tile), axis=0), axis=0, keepdims=True),
            )

        def add(n, found):
            word_ref[pl.ds(rows_ref[n], 1), :] += found[0]
            context_ref[pl.ds(cols_ref[n], 1), :] += found[1]

        def one_piece(at, carry):
            arriving(at).wait()
            over_tiles(
                piece, 32, lambda n: sums(at * piece + n), lambda n, found: add(at * piece + n, found)
            )
            return carry

        lax.fori_loop(0, pieces, one_piece, 0)

    return pl.pallas_call(
        kernel,
        in_specs=[HBM] * 3 + [ANY] * len(deps),
        out_specs=[IN_VMEM] * 2,
        out_shape=[
            jax.ShapeDtypeStruct((band_rows, tile), F32),
            jax.ShapeDtypeStruct((band_cols, tile), F32),
        ],
        scratch_shapes=[
            pltpu.VMEM(counts.shape, counts.dtype),
            pltpu.SMEM((slots,), jnp.int32),
            pltpu.SMEM((slots,), jnp.int32),
            pltpu.SemaphoreType.DMA((pieces + 2,)),
        ],
        compiler_params=params(48),
        cost_estimate=cost(0.01),
        name="count_sums",
    )(in_hbm(counts), in_hbm(rows), in_hbm(cols), *deps)


def bundles(core, word_part, contexts):
    band_rows, tile = word_part.shape
    band_cols = contexts[0].shape[0]
    half = band_rows // 2

    def kernel(core_ref, word_ref, *refs):
        keep_ref, give_ref, log_ref = refs[len(contexts) :]
        total = refs[0][...]
        for ref in refs[1 : len(contexts)]:
            total = total + ref[...]
        root = jnp.sqrt(total)
        powers = root * jnp.sqrt(root)
        power = jnp.sum(powers.reshape(band_cols // 8, 8, tile), axis=0)
        for ref, at in ((keep_ref, core_ref[0]), (give_ref, 1 - core_ref[0])):
            ref[:half] = word_ref[pl.ds(pl.multiple_of(at * half, half), half), :]
            ref[half:] = power
        log_ref[...] = jnp.maximum(0.75 * jnp.log(total), 0.0)

    return pl.pallas_call(
        kernel,
        in_specs=[IN_SMEM] + [IN_VMEM] * (1 + len(contexts)),
        out_specs=[IN_VMEM] * 3,
        out_shape=[
            jax.ShapeDtypeStruct((half + 8, tile), F32),
            jax.ShapeDtypeStruct((half + 8, tile), F32),
            jax.ShapeDtypeStruct((band_cols, tile), F32),
        ],
        compiler_params=params(16),
        name="bundles",
    )(core, word_part, *contexts)


def plus(a, b):
    def kernel(a_ref, b_ref, out_ref):
        out_ref[...] = a_ref[...] + b_ref[...]

    return pl.pallas_call(
        kernel,
        in_specs=[IN_VMEM] * 2,
        out_specs=IN_VMEM,
        out_shape=jax.ShapeDtypeStruct(a.shape, a.dtype),
        compiler_params=params(16),
        name="plus",
    )(a, b)


def turn_panel(panel, tile, group, deps):
    blocks, width = panel.shape[0] // tile, panel.shape[1]
    part = width // GROUPS

    def kernel(in_ref, *refs):
        out_ref = refs[-1]
        for n in range(blocks):
            turned = in_ref[n * tile : (n + 1) * tile, :].astype(F32).T.astype(BF16)
            out_ref[n] = turned[group * part : (group + 1) * part]

    return pl.pallas_call(
        kernel,
        in_specs=[IN_VMEM] + [ANY] * len(deps),
        out_specs=IN_VMEM,
        out_shape=jax.ShapeDtypeStruct((blocks, part, tile), BF16),
        compiler_params=params(16),
        name="turn_panel",
    )(in_hbm(panel), *deps)


def add_up(terms, count, width, dtypes, deps=(), other=None):
    tile = terms[0][0].shape[-1]
    n_terms = len(terms)

    def kernel(place_ref, *refs):
        outs = refs[n_terms + (other is not None) + len(deps) :]

        def write():
            total = refs[0][...].astype(F32)
            for ref in refs[1:n_terms]:
                total = total + ref[...].astype(F32)
            for out in outs:
                out[...] = total.astype(out.dtype)

        if other is None:
            write()
        else:
            pl.when(place_ref[0] < other[2])(write)

            @pl.when(place_ref[0] >= other[2])
            def _():
                outs[0][...] = refs[n_terms][...]

    shape = (count, width, tile)
    blocks = [pl.BlockSpec(shape, lambda n, _, at=at: (*at, 0)) for _, at in terms]
    arrays = [array for array, _ in terms]
    if other is None:
        place = jnp.zeros((1,), jnp.int32)
    else:
        place = other[1]
        blocks.append(pl.BlockSpec(shape, lambda n, _: (0, 0, 0)))
        arrays.append(other[0])
    return pl.pallas_call(
        kernel,
        grid_spec=pltpu.PrefetchScalarGridSpec(
            num_scalar_prefetch=1,
            grid=(1,),
            in_specs=blocks + [ANY] * len(deps),
            out_specs=[pl.BlockSpec(shape, lambda n, _: (0, 0, 0))] * len(dtypes),
        ),
        out_shape=[
            (pltpu.HBM if len(dtypes) > 1 and dtype == F32 else jax.ShapeDtypeStruct)(shape, dtype)
            for dtype in dtypes
        ],
        compiler_params=params(24),
        cost_estimate=cost(0.01),
        name="add_up",
    )(place, *arrays, *deps)


def word_products(index, blocks, chips, block_rows, tiles=None, source=None, deps=()):
    shape = (tiles if source is None else source[0]).shape
    slots, tile, _ = shape
    share, width, _ = blocks[0].shape
    slot_count = 2 * chips - 1
    n_in = len(blocks)
    chip_list = 3 * slots
    pieces = math.gcd(slots, 5)
    piece = slots // pieces

    def kernel(index_ref, *refs):
        if source is None:
            tiles_ref, *refs = refs
        else:
            counts_hbm, core_ref, own_ref, other_ref, log_ref, *refs = refs
        block_refs, refs = refs[:n_in], refs[n_in + len(deps) :]
        if source is not None:
            tiles_ref, *refs = refs
        outs, refs = refs[:slot_count], refs[slot_count:]
        acc, band, sems, *refs = refs
        copies = [
            pltpu.make_async_copy(ref, band.at[pl.ds(n * share, share)], sems.at[n])
            for n, ref in enumerate(block_refs)
        ]
        for copy in copies:
            copy.start()
        acc[...] = jnp.zeros_like(acc)
        if source is not None:
            word_log, shift, counts_ref, count_sems = refs

            def arriving(n):
                part = pl.ds(n * piece, piece)
                return pltpu.make_async_copy(
                    counts_hbm.at[part], counts_ref.at[part], count_sems.at[n]
                )

            for n in range(pieces):
                arriving(n).start()
            half = own_ref.shape[0] - 8
            for ref, at in ((own_ref, core_ref[0]), (other_ref, 1 - core_ref[0])):
                rows = pl.ds(pl.multiple_of(at * half, half), half)
                word_log[rows, :] = jnp.log(jnp.maximum(ref[:half], 1.0))
            power = own_ref[half:]
            power = jnp.sum(jnp.sum(power, axis=0, keepdims=True), axis=1, keepdims=True)
            shift[...] = (jnp.log(power) - math.log(NEG_SAMPLES)) - log_ref[...]
        for copy in copies:
            copy.wait()

        def product(n):
            if source is None:
                made = tiles_ref[n]
            else:
                word = word_log[pl.ds(index_ref[n], 1), :]
                word = jnp.broadcast_to(word, (tile, tile)).T
                context = shift[pl.ds(index_ref[slots + n], 1), :]
                pointwise = jnp.log(counts_ref[n].astype(F32)) + (context - word)
                made = jnp.maximum(pointwise, 0.0).astype(BF16)
                tiles_ref[n] = made
            return lax.dot_general(
                band[index_ref[2 * slots + n]],
                made,
                (((1,), (1,)), ((), ())),
                preferred_element_type=F32,
            )

        def add(n, found):
            acc[index_ref[n]] += found

        def one_piece(at, carry):
            if source is not None:
                arriving(at).wait()
            over_tiles(
                piece,
                32,
                lambda n: product(at * piece + n),
                lambda n, found: add(at * piece + n, found),
            )
            return carry

        lax.fori_loop(0, pieces, one_piece, 0)
        for slot, out in enumerate(outs):

            at = index_ref[chip_list + slot]

            @pl.when((at >= 0) & (at < chips))
            def _():
                out[...] = acc[pl.ds(at * block_rows, block_rows)].astype(out.dtype)

    out_shape = [
        pltpu.VMEM((block_rows, width, tile), BF16)
        for slot in range(slot_count)
    ]
    out_specs = [IN_VMEM] * slot_count
    scratch = [
        pltpu.VMEM((chips * block_rows, width, tile), F32),
        pltpu.VMEM((n_in * share, width, tile), BF16),
        pltpu.SemaphoreType.DMA((n_in,)),
    ]
    if source is None:
        operands, operand_specs = [tiles], [IN_VMEM]
    else:
        operands = [in_hbm(source[0]), *source[1:]]
        operand_specs = [HBM, IN_SMEM] + [IN_VMEM] * 3
    if source is not None:
        out_shape = [pltpu.VMEM(shape, BF16)] + out_shape
        out_specs = [IN_VMEM] + out_specs
        scratch += [
            pltpu.VMEM((chips * block_rows, tile), F32),
            pltpu.VMEM(source[-1].shape, F32),
            pltpu.VMEM(shape, jnp.int32),
            pltpu.SemaphoreType.DMA((pieces,)),
        ]
    outs = pl.pallas_call(
        kernel,
        in_specs=[IN_SMEM] + operand_specs + [ANY] * (n_in + len(deps)),
        out_specs=out_specs,
        out_shape=out_shape,
        scratch_shapes=scratch,
        compiler_params=params(40 if source is not None else 32),
        cost_estimate=cost(0.01),
        name="word_products" if source is None else "ppmi_word_products",
    )(index, *operands, *blocks, *deps)
    if source is not None:
        tiles, *outs = outs
    given = {distance: outs[chips - 1 - distance] for distance in range(1, chips)}
    kept = {distance: outs[chips - 1 + distance] for distance in range(1, chips)}
    return tiles, given, outs[chips - 1], kept


def context_products(index, tiles, blocks, band_cols, deps):
    slots, tile, _ = tiles.shape
    block_rows, part, _ = blocks[0][0].shape
    slot_count, parts = len(blocks), len(blocks[0])
    width = part * parts
    chips = (slot_count + 1) // 2
    half = band_cols // 2
    chip_list = 3 * slots

    def kernel(index_ref, tiles_ref, *refs):
        block_refs, refs = refs[: slot_count * parts], refs[slot_count * parts + len(deps) :]
        send, keep, acc, band, sems = refs

        def each_copy(act):
            for slot in range(slot_count):
                at = index_ref[chip_list + slot]

                @pl.when((at >= 0) & (at < chips))
                def _():
                    for n in range(parts):
                        rows, columns = pl.ds(at * block_rows, block_rows), pl.ds(n * part, part)
                        act(
                            pltpu.make_async_copy(
                                block_refs[slot * parts + n], band.at[rows, columns], sems.at[slot, n]
                            )
                        )

        each_copy(lambda copy: copy.start())
        acc[...] = jnp.zeros_like(acc)
        each_copy(lambda copy: copy.wait())

        def product(n):
            return jnp.dot(band[index_ref[n]], tiles_ref[n], preferred_element_type=F32)

        def add(n, found):
            acc[index_ref[2 * slots + n]] += found

        over_tiles(slots, 80, product, add)
        send[...] = acc[half:].astype(BF16)
        keep[...] = acc[:half]

    shape = (half, width, tile)
    return pl.pallas_call(
        kernel,
        in_specs=[IN_SMEM, IN_VMEM] + [ANY] * (slot_count * parts + len(deps)),
        out_specs=[IN_VMEM] * 2,
        out_shape=[jax.ShapeDtypeStruct(shape, BF16), jax.ShapeDtypeStruct(shape, F32)],
        scratch_shapes=[
            pltpu.VMEM((band_cols, width, tile), F32),
            pltpu.VMEM((chips * block_rows, width, tile), BF16),
            pltpu.SemaphoreType.DMA((slot_count, parts)),
        ],
        compiler_params=params(32),
        cost_estimate=cost(0.01),
        name="context_products",
    )(index, tiles, *[ref for block in blocks for ref in block], *deps)


def turn_back(pieces, start, blocks, scale, pinned=False, deps=()):
    _, _, tile = pieces[0][0].shape
    terms = [term for piece in pieces for term in piece]
    width = sum(piece[0].shape[1] for piece in pieces)
    step = math.gcd(blocks, 16)

    def kernel(start_ref, *refs):
        out_ref, reads = refs[-1], list(refs[: len(terms)])
        for n in range(step):
            columns, at = [], 0
            for piece in pieces:
                columns.append(sum(ref[n].astype(F32) for ref in reads[at : at + len(piece)]))
                at += len(piece)
            out_ref[n * tile : (n + 1) * tile, :] = jnp.concatenate(columns, axis=0).T * scale

    return pl.pallas_call(
        kernel,
        grid_spec=pltpu.PrefetchScalarGridSpec(
            num_scalar_prefetch=1,
            grid=(blocks // step,),
            in_specs=[
                pl.BlockSpec((step, term.shape[1], tile), lambda n, at: (at[0] + n, 0, 0))
                for term in terms
            ]
            + [ANY] * len(deps),
            out_specs=pl.BlockSpec((step * tile, width), lambda n, at: (n, 0)),
        ),
        out_shape=jax.ShapeDtypeStruct((blocks * tile, width), F32),
        compiler_params=params(32),
        cost_estimate=cost(0.01),
        name="turn_back",
    )(start // step, *[in_hbm(term) if pinned else term for term in terms], *deps)


def shards(n_row, n_col, tile_counts, tile_rows, tile_cols, panel):
    counts, rows, cols = tile_counts[0, 0], tile_rows[0, 0], tile_cols[0, 0]
    tile = counts.shape[-1]
    share = panel.shape[0] // tile
    band_rows, band_cols = share * n_col, share * n_row
    chips, bits = n_col // 2, n_row.bit_length() - 1
    block_rows = 2 * share
    my_row, my_col = lax.axis_index("row"), lax.axis_index("col")
    chip, core = my_col // 2, my_col % 2

    def row_swap(x, step):
        pairs = []
        for r in range(n_row):
            for c in range(n_col):
                bit = step if c % 2 == 0 else bits - 1 - step
                pairs.append((r * n_col + c, (r ^ (1 << bit)) * n_col + c))
        return lax.ppermute(x, ("row", "col"), pairs)

    def core_swap(x, keep=lambda c, z: True):
        return lax.ppermute(
            x, "col", [(i, i ^ 1) for i in range(n_col) if keep(i % 2, i // 2)]
        )

    def along(x):
        pairs = []
        for z in range(chips - 1):
            pairs.append((2 * z, 2 * z + 2))
            pairs.append((2 * (chips - 1 - z) + 1, 2 * (chips - 2 - z) + 1))
        return lax.ppermute(x, "col", pairs)

    def row_xor(x, mask):
        return lax.ppermute(x, "row", [(r, r ^ mask) for r in range(n_row)])

    def chip_xor(x, mask):
        return lax.ppermute(x, "col", [(c, c ^ (2 * mask)) for c in range(n_col)])

    sign = jnp.where(core == 0, 1, -1)
    slot_chip = (jnp.arange(2 * chips - 1, dtype=jnp.int32) - (chips - 1)) * sign + chip
    differ = (cols // share) ^ my_row
    turned = sum(((differ >> b) & 1) << (bits - 1 - b) for b in range(bits))
    col_place = jnp.where(core == 0, turned, differ) * share + cols % share
    index = jnp.concatenate([rows, cols, col_place, slot_chip])
    behind = jnp.where(core == 0, chip, chips - 1 - chip).reshape(1)

    def spread(block):
        return {0: block} | {1 << (bits - 1 - step): row_swap(block, step) for step in range(bits)}

    def spread_on(blocks, deps=None):
        blocks = dict(blocks)
        for step in range(1, bits):
            bit = 1 << (bits - 1 - step)
            for at in sorted(blocks):
                if at & -at > bit:
                    block = blocks[at]
                    if deps is not None:
                        shape = block.shape
                        (block,) = add_up([(block, (0, 0))], *shape[:2], [BF16], deps)
                    blocks[at | bit] = row_swap(block, step)
        return [blocks[at] for at in range(n_row)]

    turned_panel = turn_panel(panel, tile, 0, ())
    panel_blocks = spread_on(spread(turned_panel))

    word_part, context = count_sums(counts, rows, cols, band_rows, band_cols, (turned_panel,))
    contexts = [context] + [row_xor(context, mask) for mask in range(1, n_row)]
    this_core = core.reshape(1)
    bundle, given, context_log = bundles(this_core, word_part, contexts)
    bundle = plus(bundle, core_swap(given))
    for step in range(chips.bit_length() - 1):
        bundle = plus(bundle, chip_xor(bundle, 1 << step))

    part = panel.shape[1] // (GROUPS * PARTS)
    groups = [None] * GROUPS
    near = [[{} for _ in range(PARTS)] for _ in range(GROUPS)]
    swapped = [[{} for _ in range(PARTS)] for _ in range(GROUPS)]
    own = [[None] * PARTS for _ in range(GROUPS)]
    word_pieces, context_pieces = [], []
    stages, through = [], []
    source = (counts, this_core, bundle, core_swap(bundle), context_log)
    tiles, *groups[0] = word_products(index, panel_blocks, chips, block_rows, source=source)
    got, passed = [None] * PARTS, {}
    last = ()

    def contexts_of(group, parts, deps):
        blocks = [[near[group][n][d] for n in parts] for d in range(chips - 1, 0, -1)]
        blocks.append([own[group][n] for n in parts])
        blocks += [[swapped[group][n][d] for n in parts] for d in range(1, chips)]
        send, keep = context_products(index, tiles, blocks, band_cols, deps)
        sent = [send]
        terms, count = [(keep, 0)], band_cols // 2
        for step in range(bits):
            terms.append((row_swap(send, step), 0))
            sent.append(terms[-1][0])
            if step < bits - 1:
                count //= 2
                (send,) = add_up(
                    [(x, (2 * y + 1, 0)) for x, y in terms], count, part * len(parts), [BF16]
                )
                terms = [(x, 2 * y) for x, y in terms]
        context_pieces.append([x for x, _ in terms])
        return sent

    for slot in range(chips * GROUPS + chips - 2):
        group, step = slot // chips, slot % chips + 1
        before, hop = group - 1, step + 1
        if group < GROUPS and step < chips:
            given, mine, kept = groups[group]
            if step == 1:
                both = [(mine, (0, 0)), (core_swap(mine), (0, 0))]
            if step == 2:
                (mine_sum,) = add_up(both, block_rows, part * PARTS, [F32], last)
            far = chips - step
            passed[far] = core_swap(
                given[far], lambda c, z, far=far: z >= far if c == 0 else z < chips - far
            )
        for n in range(PARTS):
            if group < GROUPS and step == chips:
                terms = [(got[n], (0, 0)), (core_swap(got[n]), (0, 0)), (mine_sum, (0, n))]
                payload, whole = add_up(terms, block_rows, part, [BF16, F32], last)
                own[group][n] = payload
                if group and n == PARTS - 1:
                    through = contexts_of(before, range(PARTS), (payload,))
                word_pieces.append([whole])
            elif group < GROUPS:
                terms = [(kept[far], (0, n)), (passed[far], (0, n))]
                if step > 1:
                    terms.append((got[n], (0, 0)))
                other = None
                if group > 0 and hop < chips:
                    other = (near[before][n][hop - 1], behind, step)
                (payload,) = add_up(terms, block_rows, part, [BF16], last, other)
            else:
                payload = near[before][n][hop - 1]
                if through and n == (0 if step == 1 else PARTS - 1):
                    last = (*last, through[min(step - 1, bits)])
                (payload,) = add_up([(payload, (0, 0))], block_rows, part, [BF16], last)
            got[n] = along(payload)
            last = (payload,)
            if n == 0 and step == 1 and group < GROUPS - 1:
                next_blocks = spread(turn_panel(panel, tile, group + 1, last))
            if group < GROUPS and step == chips:
                arrived = (group, 1)
            elif group > 0 and hop < chips:
                arrived = (before, hop)
            else:
                continue
            if group == GROUPS and hop == chips - 1 and n > 0:
                (got[n],) = add_up([(got[n], (0, 0))], block_rows, part, [BF16], stages[:1])
            near[arrived[0]][n][arrived[1]] = got[n]
            swapped[arrived[0]][n][arrived[1]] = core_swap(got[n])
            if group == GROUPS and hop == chips - 1:
                stages = contexts_of(before, (n,), through[-1:])
        if step == 2 and group < GROUPS - 1:
            panel_blocks = spread_on(next_blocks, last)
        if step == chips - 1 and group < GROUPS - 1:
            _, *groups[group + 1] = word_products(
                index, panel_blocks, chips, block_rows, tiles=tiles, deps=last
            )
            made = (groups[group + 1][0][1],)

    deps = (stages[0],)
    word_out = turn_back(word_pieces, (core * share).reshape(1), share, 1.0, True, deps)
    zero = jnp.zeros((1,), jnp.int32)
    return word_out, turn_back(context_pieces, zero, share, 1.0 / tile)


def solution(mesh):
    in_specs = (
        P("row", "col", None, None, None),
        P("row", "col", None),
        P("row", "col", None),
        P(("col", "row"), None),
    )
    out_specs = (P(("row", "col"), None), P(("col", "row"), None))
    body = functools.partial(shards, mesh.shape["row"], mesh.shape["col"])
    return jax.shard_map(body, mesh=mesh, in_specs=in_specs, out_specs=out_specs, check_vma=False)
```

```python
import functools
import math

import jax
import jax.numpy as jnp
from jax import lax
from jax.experimental import pallas as pl
from jax.experimental.pallas import tpu as pltpu
from jax.sharding import PartitionSpec as P

NEG_SAMPLES = 15
GROUPS = 2
PARTS = 2
F32 = jnp.float32
BF16 = jnp.bfloat16

ANY = pl.BlockSpec(memory_space=pl.ANY)
HBM = pl.BlockSpec(memory_space=pltpu.HBM)
IN_VMEM = pl.BlockSpec(memory_space=pltpu.VMEM)
IN_SMEM = pl.BlockSpec(memory_space=pltpu.SMEM)


def params(mib):
    return pltpu.CompilerParams(vmem_limit_bytes=mib * 2**20)


def cost(microseconds):
    return pl.CostEstimate(flops=0, bytes_accessed=int(microseconds * 3.69e6), transcendentals=0)


def in_hbm(x):
    return pltpu.with_memory_space_constraint(x, pltpu.HBM)


def over_tiles(slots, unroll, first, second):
    unroll = math.gcd(slots, unroll)

    def body(at, carry):
        found = [first(at * unroll + n) for n in range(unroll)]
        for n, one in enumerate(found):
            second(at * unroll + n, one)
        return carry

    lax.fori_loop(0, slots // unroll, body, 0)


def count_sums(counts, rows, cols, band_rows, band_cols, deps):
    slots, tile, _ = counts.shape
    pieces = math.gcd(slots, 5)
    piece = slots // pieces

    def kernel(counts_ref, rows_hbm, cols_hbm, *refs):
        word_ref, context_ref, held, rows_ref, cols_ref, sems = refs[len(deps) :]
        lists = [
            pltpu.make_async_copy(rows_hbm, rows_ref, sems.at[pieces]),
            pltpu.make_async_copy(cols_hbm, cols_ref, sems.at[pieces + 1]),
        ]

        def arriving(n):
            part = pl.ds(n * piece, piece)
            return pltpu.make_async_copy(counts_ref.at[part], held.at[part], sems.at[n])

        for copy in lists + [arriving(n) for n in range(pieces)]:
            copy.start()
        word_ref[...] = jnp.zeros_like(word_ref)
        context_ref[...] = jnp.zeros_like(context_ref)
        for copy in lists:
            copy.wait()

        def sums(n):
            values = held[n].astype(F32)
            return (
                jnp.sum(jnp.sum(values.T.reshape(tile // 8, 8, tile), axis=0), axis=0, keepdims=True),
                jnp.sum(jnp.sum(values.reshape(tile // 8, 8, tile), axis=0), axis=0, keepdims=True),
            )

        def add(n, found):
            word_ref[pl.ds(rows_ref[n], 1), :] += found[0]
            context_ref[pl.ds(cols_ref[n], 1), :] += found[1]

        def one_piece(at, carry):
            arriving(at).wait()
            over_tiles(
                piece, 32, lambda n: sums(at * piece + n), lambda n, found: add(at * piece + n, found)
            )
            return carry

        lax.fori_loop(0, pieces, one_piece, 0)

    return pl.pallas_call(
        kernel,
        in_specs=[HBM] * 3 + [ANY] * len(deps),
        out_specs=[IN_VMEM] * 2,
        out_shape=[
            jax.ShapeDtypeStruct((band_rows, tile), F32),
            jax.ShapeDtypeStruct((band_cols, tile), F32),
        ],
        scratch_shapes=[
            pltpu.VMEM(counts.shape, counts.dtype),
            pltpu.SMEM((slots,), jnp.int32),
            pltpu.SMEM((slots,), jnp.int32),
            pltpu.SemaphoreType.DMA((pieces + 2,)),
        ],
        compiler_params=params(48),
        cost_estimate=cost(0.01),
        name="count_sums",
    )(in_hbm(counts), in_hbm(rows), in_hbm(cols), *deps)


def bundles(core, word_part, contexts):
    band_rows, tile = word_part.shape
    band_cols = contexts[0].shape[0]
    half = band_rows // 2

    def kernel(core_ref, word_ref, *refs):
        keep_ref, give_ref, log_ref = refs[len(contexts) :]
        total = refs[0][...]
        for ref in refs[1 : len(contexts)]:
            total = total + ref[...]
        root = jnp.sqrt(total)
        powers = root * jnp.sqrt(root)
        power = jnp.sum(powers.reshape(band_cols // 8, 8, tile), axis=0)
        for ref, at in ((keep_ref, core_ref[0]), (give_ref, 1 - core_ref[0])):
            ref[:half] = word_ref[pl.ds(pl.multiple_of(at * half, half), half), :]
            ref[half:] = power
        log_ref[...] = jnp.maximum(0.75 * jnp.log(total), 0.0)

    return pl.pallas_call(
        kernel,
        in_specs=[IN_SMEM] + [IN_VMEM] * (1 + len(contexts)),
        out_specs=[IN_VMEM] * 3,
        out_shape=[
            jax.ShapeDtypeStruct((half + 8, tile), F32),
            jax.ShapeDtypeStruct((half + 8, tile), F32),
            jax.ShapeDtypeStruct((band_cols, tile), F32),
        ],
        compiler_params=params(16),
        name="bundles",
    )(core, word_part, *contexts)


def plus(a, b):
    def kernel(a_ref, b_ref, out_ref):
        out_ref[...] = a_ref[...] + b_ref[...]

    return pl.pallas_call(
        kernel,
        in_specs=[IN_VMEM] * 2,
        out_specs=IN_VMEM,
        out_shape=jax.ShapeDtypeStruct(a.shape, a.dtype),
        compiler_params=params(16),
        name="plus",
    )(a, b)


def turn_panel(panel, tile, group, deps):
    blocks, width = panel.shape[0] // tile, panel.shape[1]
    part = width // GROUPS

    def kernel(in_ref, *refs):
        out_ref = refs[-1]
        for n in range(blocks):
            turned = in_ref[n * tile : (n + 1) * tile, :].astype(F32).T.astype(BF16)
            out_ref[n] = turned[group * part : (group + 1) * part]

    return pl.pallas_call(
        kernel,
        in_specs=[IN_VMEM] + [ANY] * len(deps),
        out_specs=IN_VMEM,
        out_shape=pltpu.VMEM((blocks, part, tile), BF16),
        compiler_params=params(16),
        name="turn_panel",
    )(in_hbm(panel), *deps)


def add_up(terms, count, width, dtypes, deps=(), other=None):
    tile = terms[0][0].shape[-1]
    n_terms = len(terms)

    def kernel(place_ref, *refs):
        outs = refs[n_terms + (other is not None) + len(deps) :]

        def write():
            total = refs[0][...].astype(F32)
            for ref in refs[1:n_terms]:
                total = total + ref[...].astype(F32)
            for out in outs:
                out[...] = total.astype(out.dtype)

        if other is None:
            write()
        else:
            pl.when(place_ref[0] < other[2])(write)

            @pl.when(place_ref[0] >= other[2])
            def _():
                outs[0][...] = refs[n_terms][...]

    shape = (count, width, tile)
    blocks = [pl.BlockSpec(shape, lambda n, _, at=at: (*at, 0)) for _, at in terms]
    arrays = [array for array, _ in terms]
    if other is None:
        place = jnp.zeros((1,), jnp.int32)
    else:
        place = other[1]
        blocks.append(pl.BlockSpec(shape, lambda n, _: (0, 0, 0)))
        arrays.append(other[0])
    return pl.pallas_call(
        kernel,
        grid_spec=pltpu.PrefetchScalarGridSpec(
            num_scalar_prefetch=1,
            grid=(1,),
            in_specs=blocks + [ANY] * len(deps),
            out_specs=[pl.BlockSpec(shape, lambda n, _: (0, 0, 0))] * len(dtypes),
        ),
        out_shape=[
            (pltpu.HBM if len(dtypes) > 1 and dtype == F32 else jax.ShapeDtypeStruct)(shape, dtype)
            for dtype in dtypes
        ],
        compiler_params=params(24),
        cost_estimate=cost(0.01),
        name="add_up",
    )(place, *arrays, *deps)


def word_products(index, blocks, chips, block_rows, tiles=None, source=None, deps=()):
    shape = (tiles if source is None else source[0]).shape
    slots, tile, _ = shape
    share, width, _ = blocks[0].shape
    slot_count = 2 * chips - 1
    n_in = len(blocks)
    chip_list = 3 * slots
    pieces = math.gcd(slots, 2 if source is None else 5)
    piece = slots // pieces

    def kernel(index_ref, *refs):
        if source is None:
            tiles_ref, *refs = refs
        else:
            counts_hbm, core_ref, own_ref, other_ref, log_ref, *refs = refs
        block_refs, refs = refs[:n_in], refs[n_in + len(deps) :]
        if source is not None:
            tiles_ref, *refs = refs
        outs, refs = refs[:slot_count], refs[slot_count:]
        acc, band, sems, *refs = refs
        copies = [
            pltpu.make_async_copy(ref, band.at[pl.ds(n * share, share)], sems.at[n])
            for n, ref in enumerate(block_refs)
        ]
        for copy in copies:
            copy.start()
        acc[...] = jnp.zeros_like(acc)
        if source is not None:
            word_log, shift, counts_ref, count_sems = refs

            def arriving(n):
                part = pl.ds(n * piece, piece)
                return pltpu.make_async_copy(
                    counts_hbm.at[part], counts_ref.at[part], count_sems.at[n]
                )

            for n in range(pieces):
                arriving(n).start()
            half = own_ref.shape[0] - 8
            for ref, at in ((own_ref, core_ref[0]), (other_ref, 1 - core_ref[0])):
                rows = pl.ds(pl.multiple_of(at * half, half), half)
                word_log[rows, :] = jnp.log(jnp.maximum(ref[:half], 1.0))
            power = own_ref[half:]
            power = jnp.sum(jnp.sum(power, axis=0, keepdims=True), axis=1, keepdims=True)
            shift[...] = (jnp.log(power) - math.log(NEG_SAMPLES)) - log_ref[...]
        for copy in copies:
            copy.wait()

        def product(n):
            if source is None:
                made = tiles_ref[n]
            else:
                word = word_log[pl.ds(index_ref[n], 1), :]
                word = jnp.broadcast_to(word, (tile, tile)).T
                context = shift[pl.ds(index_ref[slots + n], 1), :]
                pointwise = jnp.log(counts_ref[n].astype(F32)) + (context - word)
                made = jnp.maximum(pointwise, 0.0).astype(BF16)
                tiles_ref[n] = made
            return lax.dot_general(
                band[index_ref[2 * slots + n]],
                made,
                (((1,), (1,)), ((), ())),
                preferred_element_type=F32,
            )

        def add(n, found):
            acc[index_ref[n]] += found

        def one_piece(at, carry):
            if source is not None:
                arriving(at).wait()
            over_tiles(
                piece,
                80 if source is None else 32,
                lambda n: product(at * piece + n),
                lambda n, found: add(at * piece + n, found),
            )
            return carry

        lax.fori_loop(0, pieces, one_piece, 0)
        for slot, out in enumerate(outs):

            at = index_ref[chip_list + slot]

            @pl.when((at >= 0) & (at < chips))
            def _():
                out[...] = acc[pl.ds(at * block_rows, block_rows)].astype(out.dtype)

    out_shape = [
        pltpu.VMEM((block_rows, width, tile), BF16)
        for slot in range(slot_count)
    ]
    out_specs = [IN_VMEM] * slot_count
    scratch = [
        pltpu.VMEM((chips * block_rows, width, tile), F32),
        pltpu.VMEM((n_in * share, width, tile), BF16),
        pltpu.SemaphoreType.DMA((n_in,)),
    ]
    if source is None:
        operands, operand_specs = [tiles], [IN_VMEM]
    else:
        operands = [in_hbm(source[0]), *source[1:]]
        operand_specs = [HBM, IN_SMEM] + [IN_VMEM] * 3
    if source is not None:
        out_shape = [pltpu.VMEM(shape, BF16)] + out_shape
        out_specs = [IN_VMEM] + out_specs
        scratch += [
            pltpu.VMEM((chips * block_rows, tile), F32),
            pltpu.VMEM(source[-1].shape, F32),
            pltpu.VMEM(shape, jnp.int32),
            pltpu.SemaphoreType.DMA((pieces,)),
        ]
    outs = pl.pallas_call(
        kernel,
        in_specs=[IN_SMEM] + operand_specs + [ANY] * (n_in + len(deps)),
        out_specs=out_specs,
        out_shape=out_shape,
        scratch_shapes=scratch,
        compiler_params=params(40 if source is not None else 32),
        cost_estimate=cost(0.01),
        name="word_products" if source is None else "ppmi_word_products",
    )(index, *operands, *blocks, *deps)
    if source is not None:
        tiles, *outs = outs
    given = {distance: outs[chips - 1 - distance] for distance in range(1, chips)}
    kept = {distance: outs[chips - 1 + distance] for distance in range(1, chips)}
    return tiles, given, outs[chips - 1], kept


def context_products(index, tiles, blocks, band_cols, deps):
    slots, tile, _ = tiles.shape
    block_rows, part, _ = blocks[0][0].shape
    slot_count, parts = len(blocks), len(blocks[0])
    width = part * parts
    chips = (slot_count + 1) // 2
    half = band_cols // 2
    chip_list = 3 * slots

    def kernel(index_ref, tiles_ref, *refs):
        block_refs, refs = refs[: slot_count * parts], refs[slot_count * parts + len(deps) :]
        send, keep, acc, band, sems = refs

        def each_copy(act):
            for slot in range(slot_count):
                at = index_ref[chip_list + slot]

                @pl.when((at >= 0) & (at < chips))
                def _():
                    for n in range(parts):
                        rows, columns = pl.ds(at * block_rows, block_rows), pl.ds(n * part, part)
                        act(
                            pltpu.make_async_copy(
                                block_refs[slot * parts + n], band.at[rows, columns], sems.at[slot, n]
                            )
                        )

        each_copy(lambda copy: copy.start())
        acc[...] = jnp.zeros_like(acc)
        each_copy(lambda copy: copy.wait())

        def product(n):
            return jnp.dot(band[index_ref[n]], tiles_ref[n], preferred_element_type=F32)

        def add(n, found):
            acc[index_ref[2 * slots + n]] += found

        over_tiles(slots, 80, product, add)
        send[...] = acc[half:].astype(BF16)
        keep[...] = acc[:half]

    shape = (half, width, tile)
    return pl.pallas_call(
        kernel,
        in_specs=[IN_SMEM, IN_VMEM] + [ANY] * (slot_count * parts + len(deps)),
        out_specs=[IN_VMEM] * 2,
        out_shape=[jax.ShapeDtypeStruct(shape, BF16), jax.ShapeDtypeStruct(shape, F32)],
        scratch_shapes=[
            pltpu.VMEM((band_cols, width, tile), F32),
            pltpu.VMEM((chips * block_rows, width, tile), BF16),
            pltpu.SemaphoreType.DMA((slot_count, parts)),
        ],
        compiler_params=params(32),
        cost_estimate=cost(0.01),
        name="context_products",
    )(index, tiles, *[ref for block in blocks for ref in block], *deps)


def turn_back(pieces, start, blocks, scale, pinned=False, deps=()):
    _, _, tile = pieces[0][0].shape
    terms = [term for piece in pieces for term in piece]
    width = sum(piece[0].shape[1] for piece in pieces)
    step = math.gcd(blocks, 16)

    def kernel(start_ref, *refs):
        out_ref, reads = refs[-1], list(refs[: len(terms)])
        for n in range(step):
            columns, at = [], 0
            for piece in pieces:
                columns.append(sum(ref[n].astype(F32) for ref in reads[at : at + len(piece)]))
                at += len(piece)
            out_ref[n * tile : (n + 1) * tile, :] = jnp.concatenate(columns, axis=0).T * scale

    return pl.pallas_call(
        kernel,
        grid_spec=pltpu.PrefetchScalarGridSpec(
            num_scalar_prefetch=1,
            grid=(blocks // step,),
            in_specs=[
                pl.BlockSpec((step, term.shape[1], tile), lambda n, at: (at[0] + n, 0, 0))
                for term in terms
            ]
            + [ANY] * len(deps),
            out_specs=pl.BlockSpec((step * tile, width), lambda n, at: (n, 0)),
        ),
        out_shape=jax.ShapeDtypeStruct((blocks * tile, width), F32),
        compiler_params=params(32),
        cost_estimate=cost(0.01),
        name="turn_back",
    )(start // step, *[in_hbm(term) if pinned else term for term in terms], *deps)


def shards(n_row, n_col, tile_counts, tile_rows, tile_cols, panel):
    counts, rows, cols = tile_counts[0, 0], tile_rows[0, 0], tile_cols[0, 0]
    tile = counts.shape[-1]
    share = panel.shape[0] // tile
    band_rows, band_cols = share * n_col, share * n_row
    chips, bits = n_col // 2, n_row.bit_length() - 1
    block_rows = 2 * share
    my_row, my_col = lax.axis_index("row"), lax.axis_index("col")
    chip, core = my_col // 2, my_col % 2

    def row_swap(x, step):
        pairs = []
        for r in range(n_row):
            for c in range(n_col):
                bit = step if c % 2 == 0 else bits - 1 - step
                pairs.append((r * n_col + c, (r ^ (1 << bit)) * n_col + c))
        return lax.ppermute(x, ("row", "col"), pairs)

    def core_swap(x, keep=lambda c, z: True):
        return lax.ppermute(
            x, "col", [(i, i ^ 1) for i in range(n_col) if keep(i % 2, i // 2)]
        )

    def along(x):
        pairs = []
        for z in range(chips - 1):
            pairs.append((2 * z, 2 * z + 2))
            pairs.append((2 * (chips - 1 - z) + 1, 2 * (chips - 2 - z) + 1))
        return lax.ppermute(x, "col", pairs)

    def row_xor(x, mask):
        return lax.ppermute(x, "row", [(r, r ^ mask) for r in range(n_row)])

    def chip_xor(x, mask):
        return lax.ppermute(x, "col", [(c, c ^ (2 * mask)) for c in range(n_col)])

    sign = jnp.where(core == 0, 1, -1)
    slot_chip = (jnp.arange(2 * chips - 1, dtype=jnp.int32) - (chips - 1)) * sign + chip
    differ = (cols // share) ^ my_row
    turned = sum(((differ >> b) & 1) << (bits - 1 - b) for b in range(bits))
    col_place = jnp.where(core == 0, turned, differ) * share + cols % share
    index = jnp.concatenate([rows, cols, col_place, slot_chip])
    behind = jnp.where(core == 0, chip, chips - 1 - chip).reshape(1)

    def spread(block):
        return {0: block} | {1 << (bits - 1 - step): row_swap(block, step) for step in range(bits)}

    def spread_on(blocks, deps=None):
        blocks = dict(blocks)
        for step in range(1, bits):
            bit = 1 << (bits - 1 - step)
            for at in sorted(blocks):
                if at & -at > bit:
                    block = blocks[at]
                    if deps is not None:
                        shape = block.shape
                        (block,) = add_up([(block, (0, 0))], *shape[:2], [BF16], deps)
                    blocks[at | bit] = row_swap(block, step)
        return [blocks[at] for at in range(n_row)]

    turned_panel = turn_panel(panel, tile, 0, ())
    panel_blocks = spread_on(spread(turned_panel))

    word_part, context = count_sums(counts, rows, cols, band_rows, band_cols, (turned_panel,))
    contexts = [context] + [row_xor(context, mask) for mask in range(1, n_row)]
    this_core = core.reshape(1)
    bundle, given, context_log = bundles(this_core, word_part, contexts)
    bundle = plus(bundle, core_swap(given))
    for step in range(chips.bit_length() - 1):
        bundle = plus(bundle, chip_xor(bundle, 1 << step))

    part = panel.shape[1] // (GROUPS * PARTS)
    groups = [None] * GROUPS
    near = [[{} for _ in range(PARTS)] for _ in range(GROUPS)]
    swapped = [[{} for _ in range(PARTS)] for _ in range(GROUPS)]
    own = [[None] * PARTS for _ in range(GROUPS)]
    word_pieces, context_pieces = [], []
    stages, through = [], []
    source = (counts, this_core, bundle, core_swap(bundle), context_log)
    tiles, *groups[0] = word_products(index, panel_blocks, chips, block_rows, source=source)
    got, passed = [None] * PARTS, {}
    last = ()

    def contexts_of(group, parts, deps):
        blocks = [[near[group][n][d] for n in parts] for d in range(chips - 1, 0, -1)]
        blocks.append([own[group][n] for n in parts])
        blocks += [[swapped[group][n][d] for n in parts] for d in range(1, chips)]
        send, keep = context_products(index, tiles, blocks, band_cols, deps)
        sent = [send]
        terms, count = [(keep, 0)], band_cols // 2
        for step in range(bits):
            terms.append((row_swap(send, step), 0))
            sent.append(terms[-1][0])
            if step < bits - 1:
                count //= 2
                (send,) = add_up(
                    [(x, (2 * y + 1, 0)) for x, y in terms], count, part * len(parts), [BF16]
                )
                terms = [(x, 2 * y) for x, y in terms]
        context_pieces.append([x for x, _ in terms])
        return sent

    for slot in range(chips * GROUPS + chips - 2):
        group, step = slot // chips, slot % chips + 1
        before, hop = group - 1, step + 1
        if group < GROUPS and step < chips:
            given, mine, kept = groups[group]
            if step == 1:
                both = [(mine, (0, 0)), (core_swap(mine), (0, 0))]
            if step == 2:
                (mine_sum,) = add_up(both, block_rows, part * PARTS, [F32], last)
            far = chips - step
            passed[far] = core_swap(
                given[far], lambda c, z, far=far: z >= far if c == 0 else z < chips - far
            )
        for n in range(PARTS):
            if group < GROUPS and step == chips:
                terms = [(got[n], (0, 0)), (core_swap(got[n]), (0, 0)), (mine_sum, (0, n))]
                payload, whole = add_up(terms, block_rows, part, [BF16, F32], last)
                own[group][n] = payload
                if group and n == PARTS - 1:
                    through = contexts_of(before, range(PARTS), (payload,))
                word_pieces.append([whole])
            elif group < GROUPS:
                terms = [(kept[far], (0, n)), (passed[far], (0, n))]
                if step > 1:
                    terms.append((got[n], (0, 0)))
                other = None
                if group > 0 and hop < chips:
                    other = (near[before][n][hop - 1], behind, step)
                (payload,) = add_up(terms, block_rows, part, [BF16], last, other)
            else:
                payload = near[before][n][hop - 1]
                if through and n == (0 if step == 1 else PARTS - 1):
                    last = (*last, through[min(step - 1, bits)])
                (payload,) = add_up([(payload, (0, 0))], block_rows, part, [BF16], last)
            got[n] = along(payload)
            last = (payload,)
            if n == 0 and step == 1 and group < GROUPS - 1:
                next_blocks = spread(turn_panel(panel, tile, group + 1, last))
            if group < GROUPS and step == chips:
                arrived = (group, 1)
            elif group > 0 and hop < chips:
                arrived = (before, hop)
            else:
                continue
            if group == GROUPS and hop == chips - 1 and n > 0:
                (got[n],) = add_up([(got[n], (0, 0))], block_rows, part, [BF16], stages[:1])
            near[arrived[0]][n][arrived[1]] = got[n]
            swapped[arrived[0]][n][arrived[1]] = core_swap(got[n])
            if group == GROUPS and hop == chips - 1:
                stages = contexts_of(before, (n,), through[-1:])
        if step == 2 and group < GROUPS - 1:
            panel_blocks = spread_on(next_blocks, last)
        if step == chips - 1 and group < GROUPS - 1:
            _, *groups[group + 1] = word_products(
                index, panel_blocks, chips, block_rows, tiles=tiles, deps=last
            )
            made = (groups[group + 1][0][1],)

    deps = (stages[0],)
    word_out = turn_back(word_pieces, (core * share).reshape(1), share, 1.0, True, deps)
    zero = jnp.zeros((1,), jnp.int32)
    return word_out, turn_back(context_pieces, zero, share, 1.0 / tile)


def solution(mesh):
    in_specs = (
        P("row", "col", None, None, None),
        P("row", "col", None),
        P("row", "col", None),
        P(("col", "row"), None),
    )
    out_specs = (P(("row", "col"), None), P(("col", "row"), None))
    body = functools.partial(shards, mesh.shape["row"], mesh.shape["col"])
    return jax.shard_map(body, mesh=mesh, in_specs=in_specs, out_specs=out_specs, check_vma=False)
```

```python
import functools
import math

import jax
import jax.numpy as jnp
from jax import lax
from jax.experimental import pallas as pl
from jax.experimental.pallas import tpu as pltpu
from jax.sharding import PartitionSpec as P

NEG_SAMPLES = 15
GROUPS = 2
PARTS = 2
F32 = jnp.float32
BF16 = jnp.bfloat16

ANY = pl.BlockSpec(memory_space=pl.ANY)
HBM = pl.BlockSpec(memory_space=pltpu.HBM)
IN_VMEM = pl.BlockSpec(memory_space=pltpu.VMEM)
IN_SMEM = pl.BlockSpec(memory_space=pltpu.SMEM)


def params(mib):
    return pltpu.CompilerParams(vmem_limit_bytes=mib * 2**20)


def cost(microseconds):
    return pl.CostEstimate(flops=0, bytes_accessed=int(microseconds * 3.69e6), transcendentals=0)


def in_hbm(x):
    return pltpu.with_memory_space_constraint(x, pltpu.HBM)


def over_tiles(slots, unroll, first, second):
    unroll = math.gcd(slots, unroll)

    def body(at, carry):
        found = [first(at * unroll + n) for n in range(unroll)]
        for n, one in enumerate(found):
            second(at * unroll + n, one)
        return carry

    lax.fori_loop(0, slots // unroll, body, 0)


def count_sums(counts, rows, cols, band_rows, band_cols, deps):
    slots, tile, _ = counts.shape
    pieces = math.gcd(slots, 5)
    piece = slots // pieces

    def kernel(counts_ref, rows_hbm, cols_hbm, *refs):
        word_ref, context_ref, held, rows_ref, cols_ref, sems = refs[len(deps) :]
        lists = [
            pltpu.make_async_copy(rows_hbm, rows_ref, sems.at[pieces]),
            pltpu.make_async_copy(cols_hbm, cols_ref, sems.at[pieces + 1]),
        ]

        def arriving(n):
            part = pl.ds(n * piece, piece)
            return pltpu.make_async_copy(counts_ref.at[part], held.at[part], sems.at[n])

        for copy in lists + [arriving(n) for n in range(pieces)]:
            copy.start()
        word_ref[...] = jnp.zeros_like(word_ref)
        context_ref[...] = jnp.zeros_like(context_ref)
        for copy in lists:
            copy.wait()

        def sums(n):
            values = held[n].astype(F32)
            return (
                jnp.sum(jnp.sum(values.T.reshape(tile // 8, 8, tile), axis=0), axis=0, keepdims=True),
                jnp.sum(jnp.sum(values.reshape(tile // 8, 8, tile), axis=0), axis=0, keepdims=True),
            )

        def add(n, found):
            word_ref[pl.ds(rows_ref[n], 1), :] += found[0]
            context_ref[pl.ds(cols_ref[n], 1), :] += found[1]

        def one_piece(at, carry):
            arriving(at).wait()
            over_tiles(
                piece, 32, lambda n: sums(at * piece + n), lambda n, found: add(at * piece + n, found)
            )
            return carry

        lax.fori_loop(0, pieces, one_piece, 0)

    return pl.pallas_call(
        kernel,
        in_specs=[HBM] * 3 + [ANY] * len(deps),
        out_specs=[IN_VMEM] * 2,
        out_shape=[
            jax.ShapeDtypeStruct((band_rows, tile), F32),
            jax.ShapeDtypeStruct((band_cols, tile), F32),
        ],
        scratch_shapes=[
            pltpu.VMEM(counts.shape, counts.dtype),
            pltpu.SMEM((slots,), jnp.int32),
            pltpu.SMEM((slots,), jnp.int32),
            pltpu.SemaphoreType.DMA((pieces + 2,)),
        ],
        compiler_params=params(48),
        cost_estimate=cost(0.01),
        name="count_sums",
    )(in_hbm(counts), in_hbm(rows), in_hbm(cols), *deps)


def bundles(core, word_part, contexts):
    band_rows, tile = word_part.shape
    band_cols = contexts[0].shape[0]
    half = band_rows // 2

    def kernel(core_ref, word_ref, *refs):
        keep_ref, give_ref, log_ref = refs[len(contexts) :]
        total = refs[0][...]
        for ref in refs[1 : len(contexts)]:
            total = total + ref[...]
        root = jnp.sqrt(total)
        powers = root * jnp.sqrt(root)
        power = jnp.sum(powers.reshape(band_cols // 8, 8, tile), axis=0)
        for ref, at in ((keep_ref, core_ref[0]), (give_ref, 1 - core_ref[0])):
            ref[:half] = word_ref[pl.ds(pl.multiple_of(at * half, half), half), :]
            ref[half:] = power
        log_ref[...] = jnp.maximum(0.75 * jnp.log(total), 0.0)

    return pl.pallas_call(
        kernel,
        in_specs=[IN_SMEM] + [IN_VMEM] * (1 + len(contexts)),
        out_specs=[IN_VMEM] * 3,
        out_shape=[
            jax.ShapeDtypeStruct((half + 8, tile), F32),
            jax.ShapeDtypeStruct((half + 8, tile), F32),
            jax.ShapeDtypeStruct((band_cols, tile), F32),
        ],
        compiler_params=params(16),
        name="bundles",
    )(core, word_part, *contexts)


def plus(a, b):
    def kernel(a_ref, b_ref, out_ref):
        out_ref[...] = a_ref[...] + b_ref[...]

    return pl.pallas_call(
        kernel,
        in_specs=[IN_VMEM] * 2,
        out_specs=IN_VMEM,
        out_shape=jax.ShapeDtypeStruct(a.shape, a.dtype),
        compiler_params=params(16),
        name="plus",
    )(a, b)


def turn_panel(panel, tile, group, deps):
    blocks, width = panel.shape[0] // tile, panel.shape[1]
    part = width // GROUPS

    def kernel(in_ref, *refs):
        out_ref = refs[-1]
        for n in range(blocks):
            turned = in_ref[n * tile : (n + 1) * tile, :].astype(F32).T.astype(BF16)
            out_ref[n] = turned[group * part : (group + 1) * part]

    return pl.pallas_call(
        kernel,
        in_specs=[IN_VMEM] + [ANY] * len(deps),
        out_specs=IN_VMEM,
        out_shape=pltpu.VMEM((blocks, part, tile), BF16),
        compiler_params=params(16),
        name="turn_panel",
    )(in_hbm(panel), *deps)


def add_up(terms, count, width, dtypes, deps=(), other=None):
    tile = terms[0][0].shape[-1]
    n_terms = len(terms)

    def kernel(place_ref, *refs):
        outs = refs[n_terms + (other is not None) + len(deps) :]

        def write():
            total = refs[0][...].astype(F32)
            for ref in refs[1:n_terms]:
                total = total + ref[...].astype(F32)
            for out in outs:
                out[...] = total.astype(out.dtype)

        if other is None:
            write()
        else:
            pl.when(place_ref[0] < other[2])(write)

            @pl.when(place_ref[0] >= other[2])
            def _():
                outs[0][...] = refs[n_terms][...]

    shape = (count, width, tile)
    blocks = [pl.BlockSpec(shape, lambda n, _, at=at: (*at, 0)) for _, at in terms]
    arrays = [array for array, _ in terms]
    if other is None:
        place = jnp.zeros((1,), jnp.int32)
    else:
        place = other[1]
        blocks.append(pl.BlockSpec(shape, lambda n, _: (0, 0, 0)))
        arrays.append(other[0])
    return pl.pallas_call(
        kernel,
        grid_spec=pltpu.PrefetchScalarGridSpec(
            num_scalar_prefetch=1,
            grid=(1,),
            in_specs=blocks + [ANY] * len(deps),
            out_specs=[pl.BlockSpec(shape, lambda n, _: (0, 0, 0))] * len(dtypes),
        ),
        out_shape=[
            (pltpu.HBM if len(dtypes) > 1 and dtype == F32 else jax.ShapeDtypeStruct)(shape, dtype)
            for dtype in dtypes
        ],
        compiler_params=params(24),
        cost_estimate=cost(0.01),
        name="add_up",
    )(place, *arrays, *deps)


def word_products(index, blocks, chips, block_rows, tiles=None, source=None, deps=()):
    shape = (tiles if source is None else source[0]).shape
    slots, tile, _ = shape
    share, width, _ = blocks[0].shape
    slot_count = 2 * chips - 1
    n_in = len(blocks)
    chip_list = 3 * slots
    pieces = math.gcd(slots, 2 if source is None else 5)
    piece = slots // pieces

    def kernel(index_ref, *refs):
        if source is None:
            tiles_ref, *refs = refs
        else:
            counts_hbm, core_ref, own_ref, other_ref, log_ref, *refs = refs
        block_refs, refs = refs[:n_in], refs[n_in + len(deps) :]
        if source is not None:
            tiles_ref, *refs = refs
        outs, refs = refs[:slot_count], refs[slot_count:]
        acc, band, sems, *refs = refs
        copies = [
            pltpu.make_async_copy(ref, band.at[pl.ds(n * share, share)], sems.at[n])
            for n, ref in enumerate(block_refs)
        ]
        for copy in copies:
            copy.start()
        acc[...] = jnp.zeros_like(acc)
        if source is not None:
            word_log, shift, counts_ref, count_sems = refs

            def arriving(n):
                part = pl.ds(n * piece, piece)
                return pltpu.make_async_copy(
                    counts_hbm.at[part], counts_ref.at[part], count_sems.at[n]
                )

            for n in range(pieces):
                arriving(n).start()
            half = own_ref.shape[0] - 8
            for ref, at in ((own_ref, core_ref[0]), (other_ref, 1 - core_ref[0])):
                rows = pl.ds(pl.multiple_of(at * half, half), half)
                word_log[rows, :] = jnp.log(jnp.maximum(ref[:half], 1.0))
            power = own_ref[half:]
            power = jnp.sum(jnp.sum(power, axis=0, keepdims=True), axis=1, keepdims=True)
            shift[...] = (jnp.log(power) - math.log(NEG_SAMPLES)) - log_ref[...]
        for copy in copies:
            copy.wait()

        def product(n):
            if source is None:
                made = tiles_ref[n]
            else:
                word = word_log[pl.ds(index_ref[n], 1), :]
                word = jnp.broadcast_to(word, (tile, tile)).T
                context = shift[pl.ds(index_ref[slots + n], 1), :]
                pointwise = jnp.log(counts_ref[n].astype(F32)) + (context - word)
                made = jnp.maximum(pointwise, 0.0).astype(BF16)
                tiles_ref[n] = made
            return lax.dot_general(
                band[index_ref[2 * slots + n]],
                made,
                (((1,), (1,)), ((), ())),
                preferred_element_type=F32,
            )

        def add(n, found):
            acc[index_ref[n]] += found

        def one_piece(at, carry):
            if source is not None:
                arriving(at).wait()
            over_tiles(
                piece,
                80 if source is None else 32,
                lambda n: product(at * piece + n),
                lambda n, found: add(at * piece + n, found),
            )
            return carry

        lax.fori_loop(0, pieces, one_piece, 0)
        for slot, out in enumerate(outs):

            at = index_ref[chip_list + slot]

            @pl.when((at >= 0) & (at < chips))
            def _():
                out[...] = acc[pl.ds(at * block_rows, block_rows)].astype(out.dtype)

    out_shape = [
        pltpu.VMEM((block_rows, width, tile), BF16)
        for slot in range(slot_count)
    ]
    out_specs = [IN_VMEM] * slot_count
    scratch = [
        pltpu.VMEM((chips * block_rows, width, tile), F32),
        pltpu.VMEM((n_in * share, width, tile), BF16),
        pltpu.SemaphoreType.DMA((n_in,)),
    ]
    if source is None:
        operands, operand_specs = [tiles], [IN_VMEM]
    else:
        operands = [in_hbm(source[0]), *source[1:]]
        operand_specs = [HBM, IN_SMEM] + [IN_VMEM] * 3
    if source is not None:
        out_shape = [pltpu.VMEM(shape, BF16)] + out_shape
        out_specs = [IN_VMEM] + out_specs
        scratch += [
            pltpu.VMEM((chips * block_rows, tile), F32),
            pltpu.VMEM(source[-1].shape, F32),
            pltpu.VMEM(shape, jnp.int32),
            pltpu.SemaphoreType.DMA((pieces,)),
        ]
    outs = pl.pallas_call(
        kernel,
        in_specs=[IN_SMEM] + operand_specs + [ANY] * (n_in + len(deps)),
        out_specs=out_specs,
        out_shape=out_shape,
        scratch_shapes=scratch,
        compiler_params=params(40 if source is not None else 32),
        cost_estimate=cost(0.01),
        name="word_products" if source is None else "ppmi_word_products",
    )(index, *operands, *blocks, *deps)
    if source is not None:
        tiles, *outs = outs
    given = {distance: outs[chips - 1 - distance] for distance in range(1, chips)}
    kept = {distance: outs[chips - 1 + distance] for distance in range(1, chips)}
    return tiles, given, outs[chips - 1], kept


def context_products(index, tiles, blocks, band_cols, deps):
    slots, tile, _ = tiles.shape
    block_rows, part, _ = blocks[0][0].shape
    slot_count, parts = len(blocks), len(blocks[0])
    width = part * parts
    chips = (slot_count + 1) // 2
    half = band_cols // 2
    chip_list = 3 * slots

    def kernel(index_ref, tiles_ref, *refs):
        block_refs, refs = refs[: slot_count * parts], refs[slot_count * parts + len(deps) :]
        send, keep, acc, band, sems = refs

        def each_copy(act):
            for slot in range(slot_count):
                at = index_ref[chip_list + slot]

                @pl.when((at >= 0) & (at < chips))
                def _():
                    for n in range(parts):
                        rows, columns = pl.ds(at * block_rows, block_rows), pl.ds(n * part, part)
                        act(
                            pltpu.make_async_copy(
                                block_refs[slot * parts + n], band.at[rows, columns], sems.at[slot, n]
                            )
                        )

        each_copy(lambda copy: copy.start())
        acc[...] = jnp.zeros_like(acc)
        each_copy(lambda copy: copy.wait())

        def product(n):
            return jnp.dot(band[index_ref[n]], tiles_ref[n], preferred_element_type=F32)

        def add(n, found):
            acc[index_ref[2 * slots + n]] += found

        over_tiles(slots, 80, product, add)
        send[...] = acc[half:].astype(BF16)
        keep[...] = acc[:half]

    shape = (half, width, tile)
    return pl.pallas_call(
        kernel,
        in_specs=[IN_SMEM, IN_VMEM] + [ANY] * (slot_count * parts + len(deps)),
        out_specs=[IN_VMEM] * 2,
        out_shape=[jax.ShapeDtypeStruct(shape, BF16), jax.ShapeDtypeStruct(shape, F32)],
        scratch_shapes=[
            pltpu.VMEM((band_cols, width, tile), F32),
            pltpu.VMEM((chips * block_rows, width, tile), BF16),
            pltpu.SemaphoreType.DMA((slot_count, parts)),
        ],
        compiler_params=params(32),
        cost_estimate=cost(0.01),
        name="context_products",
    )(index, tiles, *[ref for block in blocks for ref in block], *deps)


def turn_back(pieces, start, blocks, scale, pinned=False, deps=()):
    _, _, tile = pieces[0][0].shape
    terms = [term for piece in pieces for term in piece]
    width = sum(piece[0].shape[1] for piece in pieces)
    step = math.gcd(blocks, 16)

    def kernel(start_ref, *refs):
        out_ref, reads = refs[-1], list(refs[: len(terms)])
        for n in range(step):
            columns, at = [], 0
            for piece in pieces:
                columns.append(sum(ref[n].astype(F32) for ref in reads[at : at + len(piece)]))
                at += len(piece)
            out_ref[n * tile : (n + 1) * tile, :] = jnp.concatenate(columns, axis=0).T * scale

    return pl.pallas_call(
        kernel,
        grid_spec=pltpu.PrefetchScalarGridSpec(
            num_scalar_prefetch=1,
            grid=(blocks // step,),
            in_specs=[
                pl.BlockSpec((step, term.shape[1], tile), lambda n, at: (at[0] + n, 0, 0))
                for term in terms
            ]
            + [ANY] * len(deps),
            out_specs=pl.BlockSpec((step * tile, width), lambda n, at: (n, 0)),
        ),
        out_shape=jax.ShapeDtypeStruct((blocks * tile, width), F32),
        compiler_params=params(32),
        cost_estimate=cost(0.01),
        name="turn_back",
    )(start // step, *[in_hbm(term) if pinned else term for term in terms], *deps)


def shards(n_row, n_col, tile_counts, tile_rows, tile_cols, panel):
    counts, rows, cols = tile_counts[0, 0], tile_rows[0, 0], tile_cols[0, 0]
    tile = counts.shape[-1]
    share = panel.shape[0] // tile
    band_rows, band_cols = share * n_col, share * n_row
    chips, bits = n_col // 2, n_row.bit_length() - 1
    block_rows = 2 * share
    my_row, my_col = lax.axis_index("row"), lax.axis_index("col")
    chip, core = my_col // 2, my_col % 2

    def row_swap(x, step):
        pairs = []
        for r in range(n_row):
            for c in range(n_col):
                bit = step if c % 2 == 0 else bits - 1 - step
                pairs.append((r * n_col + c, (r ^ (1 << bit)) * n_col + c))
        return lax.ppermute(x, ("row", "col"), pairs)

    def core_swap(x, keep=lambda c, z: True):
        return lax.ppermute(
            x, "col", [(i, i ^ 1) for i in range(n_col) if keep(i % 2, i // 2)]
        )

    def along(x):
        pairs = []
        for z in range(chips - 1):
            pairs.append((2 * z, 2 * z + 2))
            pairs.append((2 * (chips - 1 - z) + 1, 2 * (chips - 2 - z) + 1))
        return lax.ppermute(x, "col", pairs)

    def row_xor(x, mask):
        return lax.ppermute(x, "row", [(r, r ^ mask) for r in range(n_row)])

    def chip_xor(x, mask):
        return lax.ppermute(x, "col", [(c, c ^ (2 * mask)) for c in range(n_col)])

    sign = jnp.where(core == 0, 1, -1)
    slot_chip = (jnp.arange(2 * chips - 1, dtype=jnp.int32) - (chips - 1)) * sign + chip
    differ = (cols // share) ^ my_row
    turned = sum(((differ >> b) & 1) << (bits - 1 - b) for b in range(bits))
    col_place = jnp.where(core == 0, turned, differ) * share + cols % share
    index = jnp.concatenate([rows, cols, col_place, slot_chip])
    behind = jnp.where(core == 0, chip, chips - 1 - chip).reshape(1)

    def spread(block):
        return {0: block} | {1 << (bits - 1 - step): row_swap(block, step) for step in range(bits)}

    def spread_on(blocks, deps=None):
        blocks = dict(blocks)
        for step in range(1, bits):
            bit = 1 << (bits - 1 - step)
            for at in sorted(blocks):
                if at & -at > bit:
                    block = blocks[at]
                    if deps is not None:
                        shape = block.shape
                        (block,) = add_up([(block, (0, 0))], *shape[:2], [BF16], deps)
                    blocks[at | bit] = row_swap(block, step)
        return [blocks[at] for at in range(n_row)]

    turned_panel = turn_panel(panel, tile, 0, ())
    panel_blocks = spread_on(spread(turned_panel))

    word_part, context = count_sums(counts, rows, cols, band_rows, band_cols, (turned_panel,))
    contexts = [context] + [row_xor(context, mask) for mask in range(1, n_row)]
    this_core = core.reshape(1)
    bundle, given, context_log = bundles(this_core, word_part, contexts)
    bundle = plus(bundle, core_swap(given))
    for step in range(chips.bit_length() - 1):
        bundle = plus(bundle, chip_xor(bundle, 1 << step))

    part = panel.shape[1] // (GROUPS * PARTS)
    groups = [None] * GROUPS
    near = [[{} for _ in range(PARTS)] for _ in range(GROUPS)]
    swapped = [[{} for _ in range(PARTS)] for _ in range(GROUPS)]
    own = [[None] * PARTS for _ in range(GROUPS)]
    word_pieces, context_pieces = [], []
    stages, through = [], []
    source = (counts, this_core, bundle, core_swap(bundle), context_log)
    tiles, *groups[0] = word_products(index, panel_blocks, chips, block_rows, source=source)
    got, passed = [None] * PARTS, {}
    last = ()

    def contexts_of(group, parts, deps):
        blocks = [[near[group][n][d] for n in parts] for d in range(chips - 1, 0, -1)]
        blocks.append([own[group][n] for n in parts])
        blocks += [[swapped[group][n][d] for n in parts] for d in range(1, chips)]
        send, keep = context_products(index, tiles, blocks, band_cols, deps)
        sent = [send]
        terms, count = [(keep, 0)], band_cols // 2
        for step in range(bits):
            terms.append((row_swap(send, step), 0))
            sent.append(terms[-1][0])
            if step < bits - 1:
                count //= 2
                (send,) = add_up(
                    [(x, (2 * y + 1, 0)) for x, y in terms], count, part * len(parts), [BF16]
                )
                terms = [(x, 2 * y) for x, y in terms]
        context_pieces.append([x for x, _ in terms])
        return sent

    for slot in range(chips * GROUPS + chips - 2):
        group, step = slot // chips, slot % chips + 1
        before, hop = group - 1, step + 1
        if group < GROUPS and step < chips:
            given, mine, kept = groups[group]
            if step == 1:
                both = [(mine, (0, 0)), (core_swap(mine), (0, 0))]
            if step == 2:
                (mine_sum,) = add_up(both, block_rows, part * PARTS, [F32], last)
            far = chips - step
            passed[far] = core_swap(
                given[far], lambda c, z, far=far: z >= far if c == 0 else z < chips - far
            )
        for n in range(PARTS):
            if group < GROUPS and step == chips:
                terms = [(got[n], (0, 0)), (core_swap(got[n]), (0, 0)), (mine_sum, (0, n))]
                payload, whole = add_up(terms, block_rows, part, [BF16, F32], last)
                own[group][n] = payload
                if group and n == PARTS - 1:
                    through = contexts_of(before, range(PARTS), (payload,))
                word_pieces.append([whole])
            elif group < GROUPS:
                terms = [(kept[far], (0, n)), (passed[far], (0, n))]
                if step > 1:
                    terms.append((got[n], (0, 0)))
                other = None
                if group > 0 and hop < chips:
                    other = (near[before][n][hop - 1], behind, step)
                (payload,) = add_up(terms, block_rows, part, [BF16], last, other)
            else:
                payload = near[before][n][hop - 1]
                if through and step > 1 and n == PARTS - 1:
                    last = (*last, through[min(step - 1, bits)])
                (payload,) = add_up([(payload, (0, 0))], block_rows, part, [BF16], last)
            got[n] = along(payload)
            last = (payload,)
            if n == 0 and step == 1 and group < GROUPS - 1:
                next_blocks = spread(turn_panel(panel, tile, group + 1, last))
            if group < GROUPS and step == chips:
                arrived = (group, 1)
            elif group > 0 and hop < chips:
                arrived = (before, hop)
            else:
                continue
            if group == GROUPS and hop == chips - 1 and n > 0:
                (got[n],) = add_up([(got[n], (0, 0))], block_rows, part, [BF16], stages[:1])
            near[arrived[0]][n][arrived[1]] = got[n]
            swapped[arrived[0]][n][arrived[1]] = core_swap(got[n])
            if group == GROUPS and hop == chips - 1:
                stages = contexts_of(before, (n,), through[-1:])
        if step == 2 and group < GROUPS - 1:
            panel_blocks = spread_on(next_blocks, last)
        if step == chips - 1 and group < GROUPS - 1:
            _, *groups[group + 1] = word_products(
                index, panel_blocks, chips, block_rows, tiles=tiles, deps=last
            )
            made = (groups[group + 1][0][1],)

    deps = (stages[0],)
    word_out = turn_back(word_pieces, (core * share).reshape(1), share, 1.0, True, deps)
    zero = jnp.zeros((1,), jnp.int32)
    return word_out, turn_back(context_pieces, zero, share, 1.0 / tile)


def solution(mesh):
    in_specs = (
        P("row", "col", None, None, None),
        P("row", "col", None),
        P("row", "col", None),
        P(("col", "row"), None),
    )
    out_specs = (P(("row", "col"), None), P(("col", "row"), None))
    body = functools.partial(shards, mesh.shape["row"], mesh.shape["col"])
    return jax.shard_map(body, mesh=mesh, in_specs=in_specs, out_specs=out_specs, check_vma=False)
```
